256 devices in a mesh: section: 4 (over z_hi), dp: 64 (over y, z_lo, x, core).
Axes of the slice: x: 4, y: 4, z: 8 (z_hi: 4, z_lo: 2; z = z_hi * 2 + z_lo), core: 2. Of those that a mesh axis runs over, the one named last changes fastest.
Arguments:
- images: bfloat16 [64, 2, 64, 1664], P('dp'), may hold values from -6 to 6
- counts: int32 [64, 2], P('dp'), may hold values 0 or 1
- positions: int32 [64, 2], P('dp'), may hold values from 0 to 448, as said below
- text_rows: bfloat16 [64, 512, 4096], P('dp', None, 'section')
- norm_gain: bfloat16 [4, 1664], P('section'), may hold values from 0.25 to 1.75
- w_qkv: bfloat16 [4, 1664, 4992], P('section', 'dp'), may hold values from -4 to 4
- w_out: bfloat16 [4, 1664, 1664], P('section', 'dp'), may hold values from -0.15625 to 0.15625
- proj_gain: bfloat16 [1664], replicated, may hold values from 0.25 to 1.75
- proj_weight: bfloat16 [1664, 4096], P(None, 'section'), may hold values from -0.15625 to 0.15625
- llm_gain: bfloat16 [4096], P('section'), may hold values from 0.25 to 1.75
Outputs:
- llm_input: bfloat16 [64, 512, 4096], P('dp', None, 'section')
The draws below stay inside these ranges and needn't reach their ends.
Inputs may be any that keep to these rules, and one draw needn't show every extreme that they name: `positions`: image m's tokens lie within the m-th of 2 equal parts of the sequence.
All inputs are finite; a program needn't handle non-finite values. No bound on the sum of `counts` on one device may be relied on, other than what follows from the above.
Results may differ from the reference program's by a relative error of at most 0.012.
Values may be sent and summed in bfloat16 or wider, within the bound.
No kernel may reach another device: no remote copies, remote signals or barrier semaphores. Data moves between devices by JAX's collectives and lax.ppermute only.
A program may use at most 192 MiB of HBM per device.

```python
import jax
import jax.numpy as jnp
from jax import lax

HEADS = 13
HEAD = 128
DV = 1664
LV = 4096
PATCH = 64
MICRO = 2
SEQ = 512
LAYERS = 4
BATCH = 64


def draw_positions(key, part):
    key = jax.random.fold_in(key, 11)
    key_off, key_far, key_near = jax.random.split(key, 3)
    span = SEQ // MICRO
    offsets = jax.random.randint(key_off, (BATCH, MICRO), 0, span - PATCH + 1)
    far_row = jax.random.randint(key_far, (), 0, BATCH)
    near_row = jax.random.randint(key_near, (), 0, BATCH)
    row_ids = jnp.arange(BATCH, dtype=jnp.int32)[:, None]
    slot_ids = jnp.arange(MICRO, dtype=jnp.int32)[None, :]
    offsets = jnp.where((row_ids == near_row) & (slot_ids == 0), 0, offsets)
    offsets = jnp.where((row_ids == far_row) & (slot_ids == MICRO - 1), span - PATCH, offsets)
    starts = slot_ids * span
    return (offsets + starts).astype(jnp.int32)


def draw_text_rows(key, part):
    key = jax.random.fold_in(key, 5)
    key_base, key_rows, key_cols = jax.random.split(key, 3)
    base = jax.random.normal(key_base, (BATCH, SEQ, LV), jnp.float32)
    row_scale = jnp.exp(jax.random.uniform(key_rows, (BATCH, SEQ, 1), jnp.float32, -1.15, 1.15))
    rising = jnp.exp(jnp.arange(LV, dtype=jnp.float32) * (1.0986 / LV))
    col_scale = jnp.exp(jax.random.uniform(key_cols, (LV,), jnp.float32, -1.15, 1.15)) * rising
    return (base * row_scale * col_scale).astype(jnp.bfloat16)


def draw_images(key, part):
    key = jax.random.fold_in(key, 17)
    key_common = jax.random.fold_in(key, 0)
    return jax.random.truncated_normal(key_common, -6.0, 6.0, (BATCH, MICRO, PATCH, DV), jnp.float32).astype(jnp.bfloat16)


def draw_w_qkv(key, part):
    key = jax.random.fold_in(key, 23)
    key_base = jax.random.fold_in(key, 0)
    spread = DV ** (-0.5)
    base = jax.random.truncated_normal(key_base, -4.0, 4.0, (LAYERS, DV, 3 * DV), jnp.float32) * spread
    return base.astype(jnp.bfloat16)


def with_ends(drawn, stream_key, smallest, top_value):
    longest = drawn.shape.index(max(drawn.shape))
    spots = []
    for shift in (0, 1):
        where = [jax.random.randint(jax.random.fold_in(stream_key, axis), (), 0, length) for axis, length in enumerate(drawn.shape)]
        where[longest] = (where[longest] + shift) % drawn.shape[longest]
        spots.append(tuple(where))
    return drawn.at[spots[0]].set(smallest).at[spots[1]].set(top_value)


def steps_of(own_key, dims, pieces, least, high):
    loudness = 1.0
    for dim, blocks in pieces:
        heights = jax.random.uniform(jax.random.fold_in(jax.random.fold_in(own_key, 6), dim), (blocks,), jnp.float32, least / len(pieces), high / len(pieces))
        loudness = loudness * jnp.repeat(jnp.exp(heights), dims[dim] // blocks).reshape((-1,) + (1,) * (len(dims) - 1 - dim))
    return loudness


def centred(rng, dims, deviation, bound, shards=(), kind=jnp.bfloat16):
    drawn = jax.random.normal(rng, dims, jnp.float32) * deviation
    if len(shards) > 0:
        drawn = steps_of(rng, dims, shards, -0.22, 0.18) * drawn
    return jnp.clip(drawn, min=-bound, max=bound).astype(kind)


def setup_inputs(seed: int = 0) -> dict:
    key_of = jax.random.split(jax.random.key(seed), 11)
    images = draw_images(jax.random.fold_in(key_of[10], 71), 0)
    counts = with_ends((jax.random.randint(key_of[1], (BATCH, MICRO), 0, 4) < 3).astype(jnp.int32), jax.random.fold_in(key_of[1], 1), 0, 1)
    positions = draw_positions(jax.random.fold_in(key_of[10], 71), 0)
    text_rows = draw_text_rows(jax.random.fold_in(key_of[10], 71), 0)
    norm_gain = jnp.clip(1.0 + 0.15 * jax.random.normal(key_of[4], (LAYERS, DV), jnp.float32), 0.25, 1.75).astype(jnp.bfloat16)
    w_qkv = draw_w_qkv(jax.random.fold_in(key_of[10], 71), 0)
    w_out = centred(key_of[6], (LAYERS, DV, DV), DV ** -0.5, 0.15625, ((0, 4), (1, 64)))
    proj_gain = jnp.clip(1.0 + 0.15 * jax.random.normal(key_of[7], (DV,), jnp.float32), 0.25, 1.75).astype(jnp.bfloat16)
    proj_weight = centred(key_of[8], (DV, LV), DV ** -0.5, 0.15625, ((1, 4),))
    llm_gain = jnp.clip(1.0 + 0.15 * jax.random.normal(key_of[9], (LV,), jnp.float32), 0.25, 1.75).astype(jnp.bfloat16)
    return dict(images=images, counts=counts, positions=positions, text_rows=text_rows, norm_gain=norm_gain, w_qkv=w_qkv, w_out=w_out, proj_gain=proj_gain, proj_weight=proj_weight, llm_gain=llm_gain)


def encoder_layer(hidden, layer_gain, qkv_weight, out_weight):
    widened = hidden.astype(jnp.float32)
    normed = (widened * lax.rsqrt(lax.optimization_barrier(jnp.mean(widened * widened, -1, keepdims=True)) + 1e-06) * layer_gain.astype(jnp.float32)).astype(jnp.bfloat16)
    qkv_rows = jnp.dot(normed, qkv_weight, preferred_element_type=jnp.float32).astype(jnp.bfloat16)
    qkv_rows = qkv_rows.reshape(hidden.shape[0], 3, HEADS, HEAD).astype(jnp.float32)
    scores = jnp.einsum('qhd,khd->hqk', qkv_rows[:, 0], qkv_rows[:, 1]) * HEAD ** (-0.5)
    weights = jax.nn.softmax(scores, -1).astype(jnp.bfloat16)
    mixed = jnp.einsum('hqk,khd->qhd', weights.astype(jnp.float32), qkv_rows[:, 2]).astype(jnp.bfloat16)
    mixed = mixed.reshape(hidden.shape[0], DV)
    return (widened + jnp.dot(mixed, out_weight, preferred_element_type=jnp.float32)).astype(jnp.bfloat16)

def one_sample(images_one, counts_one, positions_one, text_one, norm_gain, w_qkv, w_out, proj_gain, proj_weight, llm_gain):
    sequence = text_one
    for slot_index in range(MICRO):
        hidden = images_one[slot_index]
        for layer_index in range(LAYERS):
            hidden = encoder_layer(hidden, norm_gain[layer_index], w_qkv[layer_index], w_out[layer_index])
        vis_float = hidden.astype(jnp.float32)
        row_mean = lax.optimization_barrier(jnp.mean(vis_float, -1, keepdims=True))
        centered = vis_float - row_mean
        row_var = lax.optimization_barrier(jnp.mean(centered * centered, -1, keepdims=True))
        normed_vis = (centered * lax.rsqrt(row_var + 1e-05) * proj_gain.astype(jnp.float32)).astype(jnp.bfloat16)
        projected = jnp.dot(normed_vis, proj_weight, preferred_element_type=jnp.float32)
        embedded = jax.nn.gelu(projected, approximate=False).astype(jnp.bfloat16)
        start = positions_one[slot_index].astype(jnp.int32)
        placed = lax.dynamic_update_slice(sequence, embedded, (start, jnp.zeros((), jnp.int32)))
        sequence = jnp.where(counts_one[slot_index] == 1, placed, sequence)
    seq_float = sequence.astype(jnp.float32)
    scale_rows = lax.rsqrt(lax.optimization_barrier(jnp.mean(seq_float * seq_float, -1, keepdims=True)) + 1e-06)
    return (seq_float * scale_rows * llm_gain.astype(jnp.float32)).astype(jnp.bfloat16)

def reference(images, counts, positions, text_rows, norm_gain, w_qkv, w_out, proj_gain, proj_weight, llm_gain):

    def per_sample(packed):
        images_one, counts_one, positions_one, text_one = packed
        return one_sample(images_one, counts_one, positions_one, text_one, norm_gain, w_qkv, w_out, proj_gain, proj_weight, llm_gain)
    return lax.map(per_sample, (images, counts, positions, text_rows))
```

```python
import jax
import jax.numpy as jnp
from jax import lax
from jax.sharding import PartitionSpec as P

HEAD = 128
LV = 4096
SECTIONS = 4
NY, NZ, NX, NC = 4, 2, 4, 2


def dp_index(y, z, x, c):
    return ((y * NZ + z) * NX + x) * NC + c


def dp_permute(array, dy=0, dz=0, dx=0, dc=0):
    pairs = []
    for y in range(NY):
        for z in range(NZ):
            for x in range(NX):
                for c in range(NC):
                    target = dp_index((y + dy) % NY, (z + dz) % NZ, (x + dx) % NX, (c + dc) % NC)
                    pairs.append((dp_index(y, z, x, c), target))
    return lax.ppermute(array, "dp", pairs)


def ring(block, axis, cut):
    before = dp_permute(block, **{axis: 1})
    after = dp_permute(block, **{axis: -1})
    far_top = dp_permute(before[:cut], **{axis: 1})
    far_low = dp_permute(after[cut:], **{axis: -1})
    return block, after, before, far_top, far_low


def in_order(blocks, place):
    own, after, before, far_top, far_low = blocks
    far = jnp.concatenate([far_top, far_low], 0)
    twice = jnp.stack([own, after, far, before, own, after, far])
    return lax.dynamic_slice_in_dim(twice, (4 - place) % 4, 4, 0).reshape(-1, own.shape[1])


def section_permute(array, pairs):
    return lax.ppermute(array, "section", pairs)


def section_sum(array):
    total = array
    for by in range(1, SECTIONS):
        total = total + section_permute(array, [(i, (i + by) % SECTIONS) for i in range(SECTIONS)])
    return total


def on_device(
    images, counts, positions, text_rows, norm_gain, w_qkv, w_out, proj_gain, proj_weight, llm_gain
):
    section = lax.axis_index("section")
    place = lax.axis_index("dp")
    core = place % NC
    x_place = (place // NC) % NX
    z_place = (place // (NC * NX)) % NZ
    y_place = place // (NC * NX * NZ)
    width = w_out.shape[2]
    heads = width // HEAD
    micro, patches = images.shape[1], images.shape[2]
    rows = micro * patches

    first = w_qkv[0][:, : 2 * width]
    second = jnp.concatenate([w_qkv[0][:, 2 * width :], w_out[0]], 1)
    is_first = core == 0
    keep = jnp.where(is_first, first, second)
    give = jnp.where(is_first, second, first)
    got = dp_permute(give, dc=1)
    pair = jnp.concatenate([jnp.where(is_first, keep, got), jnp.where(is_first, got, keep)], 0)
    other = dp_permute(pair, dz=1)
    is_low = z_place == 0
    quad = jnp.concatenate([jnp.where(is_low, pair, other), jnp.where(is_low, other, pair)], 0)
    block_a, block_b = quad[:, :width], quad[:, width:]
    ring_a = ring(block_a, "dx", 48)
    ring_b = ring(block_b, "dy", 48)
    line_a = in_order(ring_a, x_place)
    line_b = in_order(ring_b, y_place)
    half = line_a.shape[0] // 2
    mine_a = ring(line_a, "dy", half)
    mine_b = ring(line_b, "dx", half)
    swap_a = tuple(dp_permute(part, dc=1) for part in mine_a)
    swap_b = tuple(dp_permute(part, dc=1) for part in mine_b)

    text = text_rows[0].astype(jnp.float32)
    text_squares = section_sum(jnp.sum(text * text, -1))
    gain = llm_gain.astype(jnp.float32)
    out = (text * lax.rsqrt(text_squares / LV + 1e-06)[:, None] * gain).astype(jnp.bfloat16)

    def order_a(values):
        split = values.reshape(rows, NY, NZ, NX, width // (NY * NZ * NX))
        return split.transpose(1, 0, 3, 2, 4).reshape(NY, rows, width // NY)

    def order_b(values):
        split = values.reshape(rows, NY, NZ, NX, width // (NY * NZ * NX))
        return split.transpose(3, 0, 1, 2, 4).reshape(NX, rows, width // NX)

    def product(blocks, at, weights):
        own, after, before, far_top, far_low = weights

        def block(by):
            return lax.dynamic_index_in_dim(blocks, (at + by) % 4, 0, keepdims=False)

        def dot(left, right):
            return jnp.dot(left, right, preferred_element_type=jnp.float32)

        far = block(2)
        return (
            dot(block(0), own)
            + dot(block(1), after)
            + dot(block(3), before)
            + dot(far[:, :half], far_top)
            + dot(far[:, half:], far_low)
        )

    layer_gain = norm_gain[0].astype(jnp.float32)

    def layer(hidden, w_q, w_k, w_v, w_o):
        widened = hidden.astype(jnp.float32)
        normed = (
            widened * lax.rsqrt(jnp.mean(widened * widened, -1, keepdims=True) + 1e-06) * layer_gain
        ).astype(jnp.bfloat16)
        normed_a, normed_b = order_a(normed), order_b(normed)

        def by_head(values):
            return values.astype(jnp.bfloat16).reshape(micro, patches, heads, HEAD)

        query = by_head(product(normed_a, y_place, w_q))
        key = by_head(product(normed_b, x_place, w_k))
        value = by_head(product(normed_a, y_place, w_v))
        scores = jnp.einsum(
            "mqhd,mkhd->mhqk", query, key, preferred_element_type=jnp.float32
        ) * HEAD ** (-0.5)
        weights = jax.nn.softmax(scores, -1).astype(jnp.bfloat16)
        mixed = jnp.einsum("mhqk,mkhd->mqhd", weights, value, preferred_element_type=jnp.float32)
        mixed_b = order_b(mixed.astype(jnp.bfloat16).reshape(rows, width))
        return (widened + product(mixed_b, x_place, w_o)).astype(jnp.bfloat16)

    def layer_first(hidden):
        return layer(hidden, mine_a, mine_b, swap_a, swap_b)

    def layer_second(hidden):
        return layer(hidden, swap_a, swap_b, mine_a, mine_b)

    hidden = images[0].reshape(rows, width)
    for stage in range(SECTIONS):
        hidden = lax.cond(is_first, layer_first, layer_second, hidden)
        if stage + 1 < SECTIONS:
            hidden = section_permute(hidden, [(stage, stage + 1)])
    last = SECTIONS - 1
    visual = jnp.where(section == last, hidden, jnp.zeros_like(hidden))
    for target in range(last):
        visual = visual + section_permute(hidden, [(last, target)])

    vis_float = visual.astype(jnp.float32)
    row_mean = jnp.mean(vis_float, -1, keepdims=True)
    centered = vis_float - row_mean
    row_var = jnp.mean(centered * centered, -1, keepdims=True)
    normed_vis = (centered * lax.rsqrt(row_var + 1e-05) * proj_gain.astype(jnp.float32)).astype(
        jnp.bfloat16
    )
    projected = jnp.dot(normed_vis, proj_weight, preferred_element_type=jnp.float32)
    embedded = jax.nn.gelu(projected, approximate=False).astype(jnp.bfloat16).astype(jnp.float32)
    squares = section_sum(jnp.sum(embedded * embedded, -1))
    placed = (embedded * lax.rsqrt(squares / LV + 1e-06)[:, None] * gain).astype(jnp.bfloat16)
    zero = jnp.zeros((), jnp.int32)
    for slot in range(micro):
        start = positions[0, slot]
        kept = lax.dynamic_slice(out, (start, zero), (patches, out.shape[1]))
        image_rows = placed[slot * patches : (slot + 1) * patches]
        chosen = jnp.where(counts[0, slot] == 1, image_rows, kept)
        out = lax.dynamic_update_slice(out, chosen, (start, zero))
    return out[None]


def solution(mesh):
    in_specs = (
        P("dp", None, None, None),
        P("dp", None),
        P("dp", None),
        P("dp", None, "section"),
        P("section", None),
        P("section", "dp", None),
        P("section", "dp", None),
        P(),
        P(None, "section"),
        P("section"),
    )
    out_specs = P("dp", None, "section")
    return jax.shard_map(
        on_device, mesh=mesh, in_specs=in_specs, out_specs=out_specs, check_vma=False
    )
```

```python
import functools

import jax
import jax.numpy as jnp
from jax import lax
from jax.experimental import pallas as pl
from jax.experimental.pallas import tpu as pltpu
from jax.sharding import PartitionSpec as P

HEAD = 128
LV = 4096
SECTIONS = 4
NY, NZ, NX, NC = 4, 2, 4, 2


def dp_index(y, z, x, c):
    return ((y * NZ + z) * NX + x) * NC + c


def dp_permute(array, dy=0, dz=0, dx=0, dc=0):
    pairs = []
    for y in range(NY):
        for z in range(NZ):
            for x in range(NX):
                for c in range(NC):
                    target = dp_index((y + dy) % NY, (z + dz) % NZ, (x + dx) % NX, (c + dc) % NC)
                    pairs.append((dp_index(y, z, x, c), target))
    return lax.ppermute(array, "dp", pairs)


def ring(block, axis, cut):
    before = dp_permute(block, **{axis: 1})
    after = dp_permute(block, **{axis: -1})
    far_top = dp_permute(before[:cut], **{axis: 1})
    far_low = dp_permute(after[cut:], **{axis: -1})
    return block, after, before, far_top, far_low


def in_order(blocks, place):
    own, after, before, far_top, far_low = blocks
    far = jnp.concatenate([far_top, far_low], 0)
    twice = jnp.stack([own, after, far, before, own, after, far])
    return lax.dynamic_slice_in_dim(twice, (4 - place) % 4, 4, 0).reshape(-1, own.shape[1])


def section_permute(array, pairs):
    return lax.ppermute(array, "section", pairs)


def section_sum(array):
    total = array
    for by in range(1, SECTIONS):
        total = total + section_permute(array, [(i, (i + by) % SECTIONS) for i in range(SECTIONS)])
    return total


def reorder(values, order):
    size = values.shape[1] // (NY * NZ * NX)
    starts = []
    if order == "a":
        for y in range(NY):
            for x in range(NX):
                for z in range(NZ):
                    starts.append(((y * NZ + z) * NX + x) * size)
    else:
        for x in range(NX):
            for y in range(NY):
                for z in range(NZ):
                    starts.append(((y * NZ + z) * NX + x) * size)
    return jnp.concatenate([values[:, s : s + size] for s in starts], 1)


def layer_kernel(patches, hidden, gain, places, *refs):
    sources, out = refs[:20], refs[20]
    weights, query, key, value, mixed, sems = refs[21:]
    rows, width = hidden.shape
    heads = width // HEAD
    core, x_place, y_place = places[0], places[1], places[2]
    line = width // 4
    half = line // 2
    groups = [sources[i * 5 : i * 5 + 5] for i in range(4)]

    def copies(matrix, parts, place):
        own, after, before, far_top, far_low = parts
        plan = [(own, 0, 0, line), (after, 1, 0, line), (far_top, 2, 0, half)]
        plan += [(far_low, 2, half, half), (before, 3, 0, line)]
        made = []
        for at, (part, by, skip, count) in enumerate(plan):
            start = pl.multiple_of(lax.rem(place + by, 4) * line + skip, 16)
            target = weights.at[matrix, pl.ds(start, count)]
            made.append(pltpu.make_async_copy(part, target, sems.at[matrix, at]))
        return made

    where = (y_place, x_place, y_place, x_place)

    @pl.when(core == 0)
    def _():
        for matrix, group in enumerate((0, 1, 2, 3)):
            for copy in copies(matrix, groups[group], where[matrix]):
                copy.start()

    @pl.when(core != 0)
    def _():
        for matrix, group in enumerate((2, 3, 0, 1)):
            for copy in copies(matrix, groups[group], where[matrix]):
                copy.start()

    def wait(matrix):
        for copy in copies(matrix, groups[matrix], where[matrix]):
            copy.wait()

    widened = hidden[...].astype(jnp.float32)
    normed = widened * lax.rsqrt(jnp.mean(widened * widened, -1, keepdims=True) + 1e-06)
    normed = (normed * gain[...].astype(jnp.float32)).astype(jnp.bfloat16)
    normed_a, normed_b = reorder(normed, "a"), reorder(normed, "b")

    tiles = [(at, min(256, width - at)) for at in range(0, width, 256)]

    def project(matrix, left, target):
        wait(matrix)
        for at, size in tiles:
            target[:, at : at + size] = jnp.dot(
                left, weights[matrix, :, at : at + size], preferred_element_type=jnp.float32
            ).astype(jnp.bfloat16)

    project(0, normed_a, query)
    project(1, normed_b, key)
    project(2, normed_a, value)

    row_image = lax.broadcasted_iota(jnp.int32, (rows, rows), 0) // patches
    column_image = lax.broadcasted_iota(jnp.int32, (rows, rows), 1) // patches
    same = row_image == column_image
    for head in range(heads):
        at = slice(head * HEAD, head * HEAD + HEAD)
        scores = lax.dot_general(
            query[:, at], key[:, at], (((1,), (1,)), ((), ())), preferred_element_type=jnp.float32
        )
        scores = jnp.where(same, scores * HEAD ** (-0.5), -jnp.inf)
        raised = jnp.exp(scores - jnp.max(scores, -1, keepdims=True))
        shares = (raised / jnp.sum(raised, -1, keepdims=True)).astype(jnp.bfloat16)
        mixed[:, at] = jnp.dot(
            shares, value[:, at], preferred_element_type=jnp.float32
        ).astype(jnp.bfloat16)

    mixed_b = reorder(mixed[...], "b")
    wait(3)
    for at, size in tiles:
        added = jnp.dot(
            mixed_b, weights[3, :, at : at + size], preferred_element_type=jnp.float32
        )
        out[:, at : at + size] = (
            hidden[:, at : at + size].astype(jnp.float32) + added
        ).astype(jnp.bfloat16)


def run_layer(hidden, gain_row, places, matrices, patches):
    rows, width = hidden.shape
    vmem = pl.BlockSpec(memory_space=pltpu.VMEM)
    return pl.pallas_call(
        functools.partial(layer_kernel, patches),
        out_shape=jax.ShapeDtypeStruct((rows, width), jnp.bfloat16),
        in_specs=[vmem, vmem, pl.BlockSpec(memory_space=pltpu.SMEM)]
        + [pl.BlockSpec(memory_space=pl.ANY)] * len(matrices),
        out_specs=vmem,
        scratch_shapes=[pltpu.VMEM((4, width, width), jnp.bfloat16)]
        + [pltpu.VMEM((rows, width), jnp.bfloat16)] * 4
        + [pltpu.SemaphoreType.DMA((4, 5))],
        compiler_params=pltpu.CompilerParams(vmem_limit_bytes=40 * 1024 * 1024),
        cost_estimate=pl.CostEstimate(
            flops=8 * rows * width * width,
            bytes_accessed=8 * width * width,
            transcendentals=rows * rows * width // HEAD,
        ),
    )(hidden, gain_row, places, *matrices)


def on_device(
    images, counts, positions, text_rows, norm_gain, w_qkv, w_out, proj_gain, proj_weight, llm_gain
):
    section = lax.axis_index("section")
    place = lax.axis_index("dp")
    core = place % NC
    x_place = (place // NC) % NX
    z_place = (place // (NC * NX)) % NZ
    y_place = place // (NC * NX * NZ)
    width = w_out.shape[2]
    heads = width // HEAD
    micro, patches = images.shape[1], images.shape[2]
    rows = micro * patches

    first = w_qkv[0][:, : 2 * width]
    second = jnp.concatenate([w_qkv[0][:, 2 * width :], w_out[0]], 1)
    is_first = core == 0
    keep = jnp.where(is_first, first, second)
    give = jnp.where(is_first, second, first)
    got = dp_permute(give, dc=1)
    pair = jnp.concatenate([jnp.where(is_first, keep, got), jnp.where(is_first, got, keep)], 0)
    other = dp_permute(pair, dz=1)
    is_low = z_place == 0
    quad = jnp.concatenate([jnp.where(is_low, pair, other), jnp.where(is_low, other, pair)], 0)
    block_a, block_b = quad[:, :width], quad[:, width:]
    ring_a = ring(block_a, "dx", 48)
    ring_b = ring(block_b, "dy", 48)
    line_a = in_order(ring_a, x_place)
    line_b = in_order(ring_b, y_place)
    half = line_a.shape[0] // 2
    mine_a = ring(line_a, "dy", half)
    mine_b = ring(line_b, "dx", half)
    swap_a = tuple(dp_permute(part, dc=1) for part in mine_a)
    swap_b = tuple(dp_permute(part, dc=1) for part in mine_b)

    text = text_rows[0].astype(jnp.float32)
    text_squares = section_sum(jnp.sum(text * text, -1))
    gain = llm_gain.astype(jnp.float32)
    out = (text * lax.rsqrt(text_squares / LV + 1e-06)[:, None] * gain).astype(jnp.bfloat16)

    places = jnp.stack([core, x_place, y_place]).astype(jnp.int32)
    gain_row = norm_gain[0].reshape(1, width)
    matrices = mine_a + mine_b + swap_a + swap_b

    def layer(hidden):
        return run_layer(hidden, gain_row, places, matrices, patches)

    hidden = images[0].reshape(rows, width)
    for stage in range(SECTIONS):
        hidden = layer(hidden)
        if stage + 1 < SECTIONS:
            hidden = section_permute(hidden, [(stage, stage + 1)])
    last = SECTIONS - 1
    visual = jnp.where(section == last, hidden, jnp.zeros_like(hidden))
    for target in range(last):
        visual = visual + section_permute(hidden, [(last, target)])

    vis_float = visual.astype(jnp.float32)
    row_mean = jnp.mean(vis_float, -1, keepdims=True)
    centered = vis_float - row_mean
    row_var = jnp.mean(centered * centered, -1, keepdims=True)
    normed_vis = (centered * lax.rsqrt(row_var + 1e-05) * proj_gain.astype(jnp.float32)).astype(
        jnp.bfloat16
    )
    projected = jnp.dot(normed_vis, proj_weight, preferred_element_type=jnp.float32)
    embedded = jax.nn.gelu(projected, approximate=False).astype(jnp.bfloat16).astype(jnp.float32)
    squares = section_sum(jnp.sum(embedded * embedded, -1))
    placed = (embedded * lax.rsqrt(squares / LV + 1e-06)[:, None] * gain).astype(jnp.bfloat16)
    zero = jnp.zeros((), jnp.int32)
    for slot in range(micro):
        start = positions[0, slot]
        kept = lax.dynamic_slice(out, (start, zero), (patches, out.shape[1]))
        image_rows = placed[slot * patches : (slot + 1) * patches]
        chosen = jnp.where(counts[0, slot] == 1, image_rows, kept)
        out = lax.dynamic_update_slice(out, chosen, (start, zero))
    return out[None]


def solution(mesh):
    in_specs = (
        P("dp", None, None, None),
        P("dp", None),
        P("dp", None),
        P("dp", None, "section"),
        P("section", None),
        P("section", "dp", None),
        P("section", "dp", None),
        P(),
        P(None, "section"),
        P("section"),
    )
    out_specs = P("dp", None, "section")
    return jax.shard_map(
        on_device, mesh=mesh, in_specs=in_specs, out_specs=out_specs, check_vma=False
    )
```

```python
import functools

import jax
import jax.numpy as jnp
from jax import lax
from jax.experimental import pallas as pl
from jax.experimental.pallas import tpu as pltpu
from jax.sharding import PartitionSpec as P

HEAD = 128
LV = 4096
SPLIT = True
SECTIONS = 4
NY, NZ, NX, NC = 4, 2, 4, 2


def dp_index(y, z, x, c):
    return ((y * NZ + z) * NX + x) * NC + c


def dp_permute(array, dy=0, dz=0, dx=0, dc=0):
    pairs = []
    for y in range(NY):
        for z in range(NZ):
            for x in range(NX):
                for c in range(NC):
                    target = dp_index((y + dy) % NY, (z + dz) % NZ, (x + dx) % NX, (c + dc) % NC)
                    pairs.append((dp_index(y, z, x, c), target))
    return lax.ppermute(array, "dp", pairs)


def ring(block, axis, cut):
    before = dp_permute(block, **{axis: 1})
    after = dp_permute(block, **{axis: -1})
    far_top = dp_permute(before[:cut], **{axis: 1})
    far_low = dp_permute(after[cut:], **{axis: -1})
    return block, after, before, far_top, far_low


def line_kernel(places, *refs):
    blocks, lines, sems = refs[:8], refs[8:10], refs[10]
    made = []
    for which in range(2):
        for by in range(4):
            slot = lax.rem(places[1 + which] + by, 4)
            made.append(
                pltpu.make_async_copy(
                    blocks[which * 4 + by], lines[which].at[slot], sems.at[which, by]
                )
            )
    for copy in made:
        copy.start()
    for copy in made:
        copy.wait()


def gather_lines(block_a, block_b, places):
    blocks = []
    for block, axis in ((block_a, "dx"), (block_b, "dy")):
        blocks += [block] + [dp_permute(block, **{axis: by}) for by in (-1, 2, 1)]
    shape = jax.ShapeDtypeStruct((4,) + block_a.shape, block_a.dtype)
    lines = pl.pallas_call(
        line_kernel,
        out_shape=(shape, shape),
        in_specs=[pl.BlockSpec(memory_space=pltpu.SMEM)] + [pl.BlockSpec(memory_space=pl.ANY)] * 8,
        out_specs=(pl.BlockSpec(memory_space=pl.ANY),) * 2,
        scratch_shapes=[pltpu.SemaphoreType.DMA((2, 4))],
        compiler_params=pltpu.CompilerParams(vmem_limit_bytes=1024 * 1024),
        name="lines",
    )(places, *blocks)
    return tuple(line.reshape(-1, line.shape[2]) for line in lines)


def section_permute(array, pairs):
    return lax.ppermute(array, "section", pairs)


def section_sum(array):
    total = array
    for by in range(1, SECTIONS):
        total = total + section_permute(array, [(i, (i + by) % SECTIONS) for i in range(SECTIONS)])
    return total


def reorder(values, order):
    size = values.shape[1] // (NY * NZ * NX)
    starts = []
    if order == "a":
        for y in range(NY):
            for x in range(NX):
                for z in range(NZ):
                    starts.append(((y * NZ + z) * NX + x) * size)
    else:
        for x in range(NX):
            for y in range(NY):
                for z in range(NZ):
                    starts.append(((y * NZ + z) * NX + x) * size)
    return jnp.concatenate([values[:, s : s + size] for s in starts], 1)


def weights_kernel(places, *refs):
    sources, weights, sems = refs[:20], refs[20], refs[21]
    core, x_place, y_place = places[0], places[1], places[2]
    line = weights.shape[1] // 4
    half = line // 2
    groups = [sources[i * 5 : i * 5 + 5] for i in range(4)]
    where = (y_place, x_place, y_place, x_place)

    def copies(matrix, parts):
        own, after, before, far_top, far_low = parts
        plan = [(own, 0, 0, line), (after, 1, 0, line), (far_top, 2, 0, half)]
        plan += [(far_low, 2, half, half), (before, 3, 0, line)]
        made = []
        for at, (part, by, skip, count) in enumerate(plan):
            start = pl.multiple_of(lax.rem(where[matrix] + by, 4) * line + skip, 16)
            target = weights.at[matrix, pl.ds(start, count)]
            made.append(pltpu.make_async_copy(part, target, sems.at[matrix, at]))
        return made

    @pl.when(core == 0)
    def _():
        for matrix, group in enumerate((0, 1, 2, 3)):
            for copy in copies(matrix, groups[group]):
                copy.start()

    @pl.when(core != 0)
    def _():
        for matrix, group in enumerate((2, 3, 0, 1)):
            for copy in copies(matrix, groups[group]):
                copy.start()

    for matrix in range(4):
        for copy in copies(matrix, groups[matrix]):
            copy.wait()


def hold_weights(matrices, places):
    width = matrices[0].shape[1]
    return pl.pallas_call(
        weights_kernel,
        out_shape=pltpu.VMEM((4, width, width), jnp.bfloat16),
        in_specs=[pl.BlockSpec(memory_space=pltpu.SMEM)]
        + [pl.BlockSpec(memory_space=pl.ANY)] * len(matrices),
        out_specs=pl.BlockSpec(memory_space=pltpu.VMEM),
        scratch_shapes=[pltpu.SemaphoreType.DMA((4, 5))],
        compiler_params=pltpu.CompilerParams(vmem_limit_bytes=1024 * 1024),
        name="weights",
    )(places, *matrices)


def layer_kernel(patches, hidden, gain, weights, out, mixed):
    rows, width = hidden.shape
    heads = width // HEAD
    widened = hidden[...].astype(jnp.float32)
    normed = widened * lax.rsqrt(jnp.mean(widened * widened, -1, keepdims=True) + 1e-06)
    normed = (normed * gain[...].astype(jnp.float32)).astype(jnp.bfloat16)
    normed_a, normed_b = reorder(normed, "a"), reorder(normed, "b")
    tiles = [(at, min(256, width - at)) for at in range(0, width, 256)]

    def dot(left, right):
        return jnp.dot(left, right, preferred_element_type=jnp.float32)

    query, key, value = [], [], []
    for at, size in tiles:
        for matrix, left, parts in ((0, normed_a, query), (1, normed_b, key), (2, normed_a, value)):
            product = dot(left, weights[matrix, :, at : at + size]).astype(jnp.bfloat16)
            parts.extend(product[:, i : i + HEAD] for i in range(0, size, HEAD))
    scores = jnp.stack(
        [
            lax.dot_general(q, k, (((1,), (1,)), ((), ())), preferred_element_type=jnp.float32)
            for q, k in zip(query, key)
        ]
    ) * HEAD ** (-0.5)
    if rows != patches:
        row_image = lax.broadcasted_iota(jnp.int32, (rows, rows), 0) // patches
        column_image = lax.broadcasted_iota(jnp.int32, (rows, rows), 1) // patches
        scores = jnp.where((row_image == column_image)[None], scores, -jnp.inf)
    raised = jnp.exp(scores - jnp.max(scores, -1, keepdims=True))
    shares = (raised / jnp.sum(raised, -1, keepdims=True)).astype(jnp.bfloat16)
    for head in range(heads):
        mixed[:, head * HEAD : head * HEAD + HEAD] = dot(shares[head], value[head]).astype(
            jnp.bfloat16
        )
    mixed_b = reorder(mixed[...], "b")
    for at, size in tiles:
        added = dot(mixed_b, weights[3, :, at : at + size])
        out[:, at : at + size] = (
            hidden[:, at : at + size].astype(jnp.float32) + added
        ).astype(jnp.bfloat16)


def run_layer(hidden, gain_row, weights, patches):
    rows, width = hidden.shape
    vmem = pl.BlockSpec(memory_space=pltpu.VMEM)
    return pl.pallas_call(
        functools.partial(layer_kernel, patches),
        out_shape=jax.ShapeDtypeStruct((rows, width), jnp.bfloat16),
        in_specs=[vmem] * 3,
        out_specs=vmem,
        scratch_shapes=[pltpu.VMEM((rows, width), jnp.bfloat16)],
        compiler_params=pltpu.CompilerParams(vmem_limit_bytes=12 * 1024 * 1024),
        cost_estimate=pl.CostEstimate(
            flops=8 * rows * width * width,
            bytes_accessed=4 * rows * width,
            transcendentals=rows * rows * width // HEAD,
        ),
        name="layer",
    )(hidden, gain_row, weights)


def diagonal(size):
    row = lax.broadcasted_iota(jnp.int32, (size, size), 0)
    return row == lax.broadcasted_iota(jnp.int32, (size, size), 1)


def embed_kernel(visual, gain, weight, embedded, squares):
    rows, columns = embedded.shape
    values = visual[...].astype(jnp.float32)
    centered = values - jnp.mean(values, -1, keepdims=True)
    variance = jnp.mean(centered * centered, -1, keepdims=True)
    normed = centered * lax.rsqrt(variance + 1e-05) * gain[...].astype(jnp.float32)
    normed = normed.astype(jnp.bfloat16)
    total = jnp.zeros((rows, 1), jnp.float32)
    for at in range(0, columns, 256):
        projected = jnp.dot(
            normed, weight[:, at : at + 256], preferred_element_type=jnp.float32
        )
        part = (0.5 * projected * (1.0 + lax.erf(projected * 0.5**0.5))).astype(jnp.bfloat16)
        embedded[:, at : at + 256] = part
        part = part.astype(jnp.float32)
        total = total + jnp.sum(part * part, -1, keepdims=True)
    squares[...] = jnp.sum(jnp.where(diagonal(rows), total, 0.0), 0, keepdims=True)


def run_embed(visual, gain_row, weight):
    rows, columns = visual.shape[0], weight.shape[1]
    vmem = pl.BlockSpec(memory_space=pltpu.VMEM)
    return pl.pallas_call(
        embed_kernel,
        out_shape=(
            jax.ShapeDtypeStruct((rows, columns), jnp.bfloat16),
            jax.ShapeDtypeStruct((1, rows), jnp.float32),
        ),
        in_specs=[vmem] * 3,
        out_specs=(vmem, vmem),
        compiler_params=pltpu.CompilerParams(vmem_limit_bytes=12 * 1024 * 1024),
        name="embed",
    )(visual, gain_row, weight)


def place_kernel(patches, positions, counts, text, embedded, gain, *refs):
    squares, out = refs[:-1], refs[-1]
    length = text.shape[0]
    rows = embedded.shape[0]
    total = squares[0][...]
    for part in squares[1:]:
        total = total + part[...]
    column = jnp.sum(jnp.where(diagonal(rows), total, 0.0), 1, keepdims=True)
    scaled = embedded[...].astype(jnp.float32) * lax.rsqrt(column / LV + 1e-06)
    scaled = (scaled * gain[...].astype(jnp.float32)).astype(jnp.bfloat16)
    at = lax.broadcasted_iota(jnp.int32, (length, patches), 0)
    patch = lax.broadcasted_iota(jnp.int32, (length, patches), 1)
    one_row = lax.broadcasted_iota(jnp.int32, (length, 1), 0)
    picks, taken = [], None
    for slot in range(rows // patches):
        start, here = positions[0, slot], counts[0, slot] == 1
        picks.append(jnp.where((at == patch + start) & here, 1.0, 0.0).astype(jnp.bfloat16))
        inside = (one_row >= start) & (one_row < start + patches) & here
        taken = inside if taken is None else taken | inside
    placed = jnp.dot(
        jnp.concatenate(picks, 1), scaled, preferred_element_type=jnp.float32
    ).astype(jnp.bfloat16)
    out[...] = jnp.where(taken, placed, text[...])


def run_place(positions, counts, text, embedded, gain_row, squares, patches):
    vmem = pl.BlockSpec(memory_space=pltpu.VMEM)
    smem = pl.BlockSpec(memory_space=pltpu.SMEM)
    return pl.pallas_call(
        functools.partial(place_kernel, patches),
        out_shape=jax.ShapeDtypeStruct(text.shape, jnp.bfloat16),
        in_specs=[smem, smem] + [vmem] * (3 + len(squares)),
        out_specs=vmem,
        compiler_params=pltpu.CompilerParams(vmem_limit_bytes=12 * 1024 * 1024),
        name="place",
    )(positions, counts, text, embedded, gain_row, *squares)


def on_device(
    images, counts, positions, text_rows, norm_gain, w_qkv, w_out, proj_gain, proj_weight, llm_gain
):
    section = lax.axis_index("section")
    place = lax.axis_index("dp")
    core = place % NC
    x_place = (place // NC) % NX
    z_place = (place // (NC * NX)) % NZ
    y_place = place // (NC * NX * NZ)
    width = w_out.shape[2]
    heads = width // HEAD
    micro, patches = images.shape[1], images.shape[2]
    rows = micro * patches

    places = jnp.stack([core, x_place, y_place]).astype(jnp.int32)

    text = text_rows[0].astype(jnp.float32)
    gain = llm_gain.astype(jnp.float32)
    text_squares = section_sum(jnp.sum(text * text, -1))

    is_first = core == 0
    is_low = z_place == 0
    parts = [w_qkv[0][:, i * width : (i + 1) * width] for i in range(3)] + [w_out[0]]
    keep = jnp.concatenate([jnp.where(is_first, parts[i], parts[i + 2]) for i in (0, 1)], 1)
    give = jnp.concatenate([jnp.where(is_first, parts[i + 2], parts[i]) for i in (0, 1)], 1)
    got = dp_permute(give, dc=1)
    pair = jnp.concatenate([jnp.where(is_first, keep, got), jnp.where(is_first, got, keep)], 0)
    other = dp_permute(pair, dz=1)
    quad = jnp.concatenate([jnp.where(is_low, pair, other), jnp.where(is_low, other, pair)], 0)
    quad, text_squares = lax.optimization_barrier((quad, text_squares))
    line_a, line_b = gather_lines(quad[:, :width], quad[:, width:], places)
    text_normed = (text * lax.rsqrt(text_squares / LV + 1e-06)[:, None] * gain).astype(jnp.bfloat16)
    half = line_a.shape[0] // 2
    mine_a = ring(line_a, "dy", half)
    mine_b = ring(line_b, "dx", half)
    swap_a = tuple(dp_permute(part, dc=1) for part in mine_a)
    swap_b = tuple(dp_permute(part, dc=1) for part in mine_b)
    weights = hold_weights(mine_a + mine_b + swap_a + swap_b, places)

    gain_row = norm_gain[0].reshape(1, width)
    pieces = [images[0, i] for i in range(micro)] if SPLIT else [images[0].reshape(rows, width)]
    last = SECTIONS - 1
    for stage in range(SECTIONS):
        moved = []
        for hidden in pieces:
            hidden = run_layer(hidden, gain_row, weights, patches)
            if stage < last:
                moved.append(section_permute(hidden, [(stage, stage + 1)]))
            else:
                visual = jnp.where(section == last, hidden, jnp.zeros_like(hidden))
                for target in range(last):
                    visual = visual + section_permute(hidden, [(last, target)])
                moved.append(visual)
        pieces = moved
    visual = jnp.concatenate(pieces, 0)
    embedded, squares = run_embed(visual, proj_gain.reshape(1, width), proj_weight)
    others = [
        section_permute(squares, [(i, (i + by) % SECTIONS) for i in range(SECTIONS)])
        for by in range(1, SECTIONS)
    ]
    out = run_place(
        positions, counts, text_normed, embedded, llm_gain.reshape(1, -1), [squares] + others, patches
    )
    return out[None]


def solution(mesh):
    in_specs = (
        P("dp", None, None, None),
        P("dp", None),
        P("dp", None),
        P("dp", None, "section"),
        P("section", None),
        P("section", "dp", None),
        P("section", "dp", None),
        P(),
        P(None, "section"),
        P("section"),
    )
    out_specs = P("dp", None, "section")
    return jax.shard_map(
        on_device, mesh=mesh, in_specs=in_specs, out_specs=out_specs, check_vma=False
    )
```

```python
import functools

import jax
import jax.numpy as jnp
from jax import lax
from jax.experimental import pallas as pl
from jax.experimental.pallas import tpu as pltpu
from jax.sharding import PartitionSpec as P

HEAD = 128
LV = 4096
SECTIONS = 4
NY, NZ, NX, NC = 4, 2, 4, 2


def dp_index(y, z, x, c):
    return ((y * NZ + z) * NX + x) * NC + c


def dp_permute(array, dy=0, dz=0, dx=0, dc=0):
    pairs = []
    for y in range(NY):
        for z in range(NZ):
            for x in range(NX):
                for c in range(NC):
                    target = dp_index((y + dy) % NY, (z + dz) % NZ, (x + dx) % NX, (c + dc) % NC)
                    pairs.append((dp_index(y, z, x, c), target))
    return lax.ppermute(array, "dp", pairs)


def ring(block, axis, first, second):
    before = dp_permute(block, **{axis: 1})
    after = dp_permute(block, **{axis: -1})
    far_first = dp_permute(before[first], **{axis: 1})
    far_second = dp_permute(after[second], **{axis: -1})
    return block, after, before, far_first, far_second


def line_kernel(places, *refs):
    blocks, lines, sems = refs[:10], refs[10:12], refs[12]
    made = []
    for which in range(2):
        own, after, before, far_first, far_second = blocks[which * 5 : which * 5 + 5]
        cut = far_first.shape[1]
        plan = [(own, 0, None), (after, 1, None), (before, 3, None)]
        plan += [(far_first, 2, pl.ds(0, cut)), (far_second, 2, pl.ds(cut, far_second.shape[1]))]
        for at, (block, by, columns) in enumerate(plan):
            target = lines[which].at[lax.rem(places[1 + which] + by, 4)]
            if columns is not None:
                target = target.at[:, columns]
            made.append(pltpu.make_async_copy(block, target, sems.at[which, at]))
    for copy in made:
        copy.start()
    for copy in made:
        copy.wait()


def gather_lines(block_a, block_b, places):
    cut = block_a.shape[1] // HEAD // 2 * HEAD
    parts = ((slice(None), slice(0, cut)), (slice(None), slice(cut, None)))
    blocks = ring(block_a, "dx", *parts) + ring(block_b, "dy", *parts)
    shape = jax.ShapeDtypeStruct((4,) + block_a.shape, block_a.dtype)
    lines = pl.pallas_call(
        line_kernel,
        out_shape=(shape, shape),
        in_specs=[pl.BlockSpec(memory_space=pltpu.SMEM)] + [pl.BlockSpec(memory_space=pl.ANY)] * 10,
        out_specs=(pl.BlockSpec(memory_space=pl.ANY),) * 2,
        scratch_shapes=[pltpu.SemaphoreType.DMA((2, 5))],
        compiler_params=pltpu.CompilerParams(vmem_limit_bytes=1024 * 1024),
        name="lines",
    )(places, *blocks)
    return tuple(line.reshape(-1, line.shape[2]) for line in lines)


def section_permute(array, pairs):
    return lax.ppermute(array, "section", pairs)


def reorder(values, order):
    size = values.shape[1] // (NY * NZ * NX)
    starts = []
    if order == "a":
        for y in range(NY):
            for x in range(NX):
                for z in range(NZ):
                    starts.append(((y * NZ + z) * NX + x) * size)
    else:
        for x in range(NX):
            for y in range(NY):
                for z in range(NZ):
                    starts.append(((y * NZ + z) * NX + x) * size)
    return jnp.concatenate([values[:, s : s + size] for s in starts], 1)


def weights_kernel(plan, places, *refs):
    count = 4 * len(plan)
    sources, weights, sems = refs[:count], refs[-2], refs[-1]
    core, x_place, y_place = places[0], places[1], places[2]
    line = weights.shape[1] // 4
    groups = [sources[i * len(plan) : (i + 1) * len(plan)] for i in range(4)]
    where = (y_place, x_place, y_place, x_place)

    def copies(matrix, parts):
        made = []
        for at, (part, (by, skip, rows)) in enumerate(zip(parts, plan)):
            start = pl.multiple_of(lax.rem(where[matrix] + by, 4) * line + skip, 16)
            target = weights.at[matrix, pl.ds(start, rows)]
            made.append(pltpu.make_async_copy(part, target, sems.at[matrix, at]))
        return made

    @pl.when(core == 0)
    def _():
        for matrix, group in enumerate((0, 1, 2, 3)):
            for copy in copies(matrix, groups[group]):
                copy.start()

    @pl.when(core != 0)
    def _():
        for matrix, group in enumerate((2, 3, 0, 1)):
            for copy in copies(matrix, groups[group]):
                copy.start()

    for matrix in range(4):
        for copy in copies(matrix, groups[matrix]):
            copy.wait()


def hold_weights(blocks, plan, places, held=None):
    width = blocks[0].shape[1]
    anywhere = pl.BlockSpec(memory_space=pl.ANY)
    vmem = pl.BlockSpec(memory_space=pltpu.VMEM)
    more = () if held is None else (pltpu.with_memory_space_constraint(held, pltpu.VMEM),)
    return pl.pallas_call(
        functools.partial(weights_kernel, plan),
        out_shape=pltpu.VMEM((4, width, width), jnp.bfloat16),
        in_specs=[pl.BlockSpec(memory_space=pltpu.SMEM)]
        + [anywhere] * len(blocks)
        + [vmem] * len(more),
        out_specs=vmem,
        input_output_aliases={1 + len(blocks): 0} if more else {},
        scratch_shapes=[pltpu.SemaphoreType.DMA((4, len(plan)))],
        compiler_params=pltpu.CompilerParams(vmem_limit_bytes=1024 * 1024),
        name="weights",
    )(places, *blocks, *more)


def first_layer_kernel(patches, places, hidden, gain, weights, out, mixed):
    @pl.when(places[3] == 0)
    def _():
        layer_kernel(patches, hidden, gain, weights, out, mixed)

    @pl.when(places[3] != 0)
    def _():
        out[...] = jnp.zeros_like(out)


def layer_kernel(patches, hidden, gain, weights, out, mixed):
    rows, width = hidden.shape
    heads = width // HEAD
    widened = hidden[...].astype(jnp.float32)
    normed = widened * lax.rsqrt(jnp.mean(widened * widened, -1, keepdims=True) + 1e-06)
    normed = (normed * gain[...].astype(jnp.float32)).astype(jnp.bfloat16)
    normed_a, normed_b = reorder(normed, "a"), reorder(normed, "b")
    tiles = [(at, min(256, width - at)) for at in range(0, width, 256)]

    def dot(left, right):
        return jnp.dot(left, right, preferred_element_type=jnp.float32)

    query, key, value = [], [], []
    for at, size in tiles:
        for matrix, left, parts in ((0, normed_a, query), (1, normed_b, key), (2, normed_a, value)):
            product = dot(left, weights[matrix, :, at : at + size]).astype(jnp.bfloat16)
            parts.extend(product[:, i : i + HEAD] for i in range(0, size, HEAD))
    scores = jnp.stack(
        [
            lax.dot_general(q, k, (((1,), (1,)), ((), ())), preferred_element_type=jnp.float32)
            for q, k in zip(query, key)
        ]
    ) * HEAD ** (-0.5)
    if rows != patches:
        row_image = lax.broadcasted_iota(jnp.int32, (rows, rows), 0) // patches
        column_image = lax.broadcasted_iota(jnp.int32, (rows, rows), 1) // patches
        scores = jnp.where((row_image == column_image)[None], scores, -jnp.inf)
    raised = jnp.exp(scores - jnp.max(scores, -1, keepdims=True))
    shares = (raised / jnp.sum(raised, -1, keepdims=True)).astype(jnp.bfloat16)
    for head in range(heads):
        mixed[:, head * HEAD : head * HEAD + HEAD] = dot(shares[head], value[head]).astype(
            jnp.bfloat16
        )
    mixed_b = reorder(mixed[...], "b")
    for at, size in tiles:
        added = dot(mixed_b, weights[3, :, at : at + size])
        out[:, at : at + size] = (
            hidden[:, at : at + size].astype(jnp.float32) + added
        ).astype(jnp.bfloat16)


def run_layer(stage, places, hidden, gain_row, weights, patches):
    rows, width = hidden.shape
    vmem = pl.BlockSpec(memory_space=pltpu.VMEM)
    weights = pltpu.with_memory_space_constraint(weights, pltpu.VMEM)
    kernel = first_layer_kernel if stage == 0 else layer_kernel
    scalars = (places,) if stage == 0 else ()
    return pl.pallas_call(
        functools.partial(kernel, patches),
        out_shape=jax.ShapeDtypeStruct((rows, width), jnp.bfloat16),
        in_specs=[pl.BlockSpec(memory_space=pltpu.SMEM)] * len(scalars) + [vmem] * 3,
        out_specs=vmem,
        scratch_shapes=[pltpu.VMEM((rows, width), jnp.bfloat16)],
        compiler_params=pltpu.CompilerParams(vmem_limit_bytes=12 * 1024 * 1024),
        cost_estimate=pl.CostEstimate(
            flops=8 * rows * width * width,
            bytes_accessed=4 * rows * width,
            transcendentals=rows * rows * width // HEAD,
        ),
        name="layer",
    )(*scalars, hidden, gain_row, weights)


def diagonal(size):
    row = lax.broadcasted_iota(jnp.int32, (size, size), 0)
    return row == lax.broadcasted_iota(jnp.int32, (size, size), 1)


def embed_kernel(spans, places, gain, weight, text_squares, *refs):
    parts, (embedded, squares) = refs[:-2], refs[-2:]
    rows, columns = embedded.shape
    values = []
    for first, count in spans:
        own, left, right, *forwarded = (part[...] for part in parts[first : first + count])
        halves = jnp.concatenate(forwarded, 0)
        total = jnp.where(places[3] == 0, left, jnp.where(places[3] == 1, halves, right))
        values.append(jnp.where(places[3] == SECTIONS - 1, own, total).astype(jnp.float32))
    values = jnp.concatenate(values, 0)
    centered = values - jnp.mean(values, -1, keepdims=True)
    variance = jnp.mean(centered * centered, -1, keepdims=True)
    normed = centered * lax.rsqrt(variance + 1e-05) * gain[...].astype(jnp.float32)
    normed = normed.astype(jnp.bfloat16)
    total = jnp.zeros((rows, 1), jnp.float32)
    for at in range(0, columns, 256):
        projected = jnp.dot(
            normed, weight[:, at : at + 256], preferred_element_type=jnp.float32
        )
        part = (0.5 * projected * (1.0 + lax.erf(projected * 0.5**0.5))).astype(jnp.bfloat16)
        embedded[:, at : at + 256] = part
        part = part.astype(jnp.float32)
        total = total + jnp.sum(part * part, -1, keepdims=True)
    squares[:, :rows] = jnp.sum(jnp.where(diagonal(rows), total, 0.0), 0, keepdims=True)
    squares[:, rows:] = text_squares[...]


def run_embed(places, pieces, gain_row, weight, text_squares):
    rows, columns = sum(piece[0].shape[0] for piece in pieces), weight.shape[1]
    parts = sum(pieces, ())
    firsts = [sum(len(piece) for piece in pieces[:i]) for i in range(len(pieces))]
    spans = [(first, len(piece)) for first, piece in zip(firsts, pieces)]
    vmem = pl.BlockSpec(memory_space=pltpu.VMEM)
    return pl.pallas_call(
        functools.partial(embed_kernel, spans),
        out_shape=(
            jax.ShapeDtypeStruct((rows, columns), jnp.bfloat16),
            jax.ShapeDtypeStruct((1, rows + text_squares.shape[1]), jnp.float32),
        ),
        in_specs=[pl.BlockSpec(memory_space=pltpu.SMEM)] + [vmem] * (3 + len(parts)),
        out_specs=(vmem, vmem),
        compiler_params=pltpu.CompilerParams(vmem_limit_bytes=12 * 1024 * 1024),
        name="embed",
    )(places, gain_row, weight, text_squares, *parts)


def place_kernel(patches, positions, counts, text, embedded, gain, *refs):
    squares, out = refs[:-1], refs[-1]
    length = text.shape[0]
    rows = embedded.shape[0]
    total = squares[0][...]
    for part in squares[1:]:
        total = total + part[...]
    scales = lax.rsqrt(total / LV + 1e-06)
    columns = []
    for first in range(0, scales.shape[1], rows):
        part = jnp.where(diagonal(rows), scales[:, first : first + rows], 0.0)
        columns.append(jnp.sum(part, 1, keepdims=True))
    gain_row = gain[...].astype(jnp.float32)

    def scale(values, column):
        return (values.astype(jnp.float32) * column * gain_row).astype(jnp.bfloat16)

    scaled = scale(embedded[...], columns[0])
    at = lax.broadcasted_iota(jnp.int32, (length, patches), 0)
    patch = lax.broadcasted_iota(jnp.int32, (length, patches), 1)
    one_row = lax.broadcasted_iota(jnp.int32, (length, 1), 0)
    picks, taken = [], None
    for slot in range(rows // patches):
        start, here = positions[0, slot], counts[0, slot] == 1
        picks.append(jnp.where((at == patch + start) & here, 1.0, 0.0).astype(jnp.bfloat16))
        inside = (one_row >= start) & (one_row < start + patches) & here
        taken = inside if taken is None else taken | inside
    placed = jnp.dot(
        jnp.concatenate(picks, 1), scaled, preferred_element_type=jnp.float32
    ).astype(jnp.bfloat16)
    out[...] = jnp.where(taken, placed, scale(text[...], jnp.concatenate(columns[1:], 0)))


def run_place(positions, counts, text, embedded, gain_row, squares, patches):
    vmem = pl.BlockSpec(memory_space=pltpu.VMEM)
    smem = pl.BlockSpec(memory_space=pltpu.SMEM)
    return pl.pallas_call(
        functools.partial(place_kernel, patches),
        out_shape=jax.ShapeDtypeStruct(text.shape, jnp.bfloat16),
        in_specs=[smem, smem] + [vmem] * (3 + len(squares)),
        out_specs=vmem,
        compiler_params=pltpu.CompilerParams(vmem_limit_bytes=12 * 1024 * 1024),
        name="place",
    )(positions, counts, text, embedded, gain_row, *squares)


def on_device(
    images, counts, positions, text_rows, norm_gain, w_qkv, w_out, proj_gain, proj_weight, llm_gain
):
    section = lax.axis_index("section")
    place = lax.axis_index("dp")
    core = place % NC
    x_place = (place // NC) % NX
    z_place = (place // (NC * NX)) % NZ
    y_place = place // (NC * NX * NZ)
    width = w_out.shape[2]
    micro, patches = images.shape[1], images.shape[2]

    places = jnp.stack([core, x_place, y_place, section]).astype(jnp.int32)

    text = text_rows[0].astype(jnp.float32)
    text_squares = jnp.sum(text * text, -1)[None]

    is_first = core == 0
    is_low = z_place == 0
    parts = [w_qkv[0][:, i * width : (i + 1) * width] for i in range(3)] + [w_out[0]]
    keep = jnp.concatenate([jnp.where(is_first, parts[i], parts[i + 2]) for i in (0, 1)], 1)
    give = jnp.concatenate([jnp.where(is_first, parts[i + 2], parts[i]) for i in (0, 1)], 1)
    got = dp_permute(give, dc=1)
    pair = jnp.concatenate([jnp.where(is_first, keep, got), jnp.where(is_first, got, keep)], 0)
    other = dp_permute(pair, dz=1)
    quad = jnp.concatenate([jnp.where(is_low, pair, other), jnp.where(is_low, other, pair)], 0)
    line_a, line_b = gather_lines(quad[:, :width], quad[:, width:], places)
    half = line_a.shape[0] // 2
    top, low = slice(0, half), slice(half, None)
    mine = (ring(line_a, "dy", top, low), ring(line_b, "dx", top, low))
    early = [images[0, i] for i in range(micro)]
    early += [norm_gain[0].reshape(1, width), proj_gain.reshape(1, width), llm_gain.reshape(1, -1)]
    places, text_squares, *early = lax.optimization_barrier((places, text_squares, *early))
    pieces, (gain_row, proj_gain_row, llm_gain_row) = early[:micro], early[micro:]
    near = sum((part[:3] for part in mine), ())
    near = near + tuple(dp_permute(part, dc=1) for part in near)
    line = line_a.shape[0]
    weights = hold_weights(near, ((0, 0, line), (1, 0, line), (3, 0, line)), places)
    far = sum((part[3:] for part in mine), ())
    far, weights = lax.optimization_barrier((far, weights))
    far = far + tuple(dp_permute(part, dc=1) for part in far)
    weights = hold_weights(far, ((2, 0, half), (2, half, half)), places, weights)

    last = SECTIONS - 1
    for stage in range(SECTIONS):
        moved = []
        for hidden in pieces:
            hidden = run_layer(stage, places, hidden, gain_row, weights, patches)
            if stage < last:
                moved.append(section_permute(hidden, [(stage, stage + 1)]))
            else:
                left = section_permute(hidden, [(last, 0)])
                right = section_permute(hidden, [(last, last - 1)])
                moved.append((hidden, left, right))
        pieces = moved
    finished = pieces[-1][0]
    for i, (hidden, left, right) in enumerate(pieces):
        left, right, finished = lax.optimization_barrier((left, right, finished))
        if i + 1 < micro:
            forwarded = (section_permute(right, [(last - 1, 1)]),)
        else:
            cut = hidden.shape[0] // 2
            top = section_permute(left[:cut], [(0, 1)])
            forwarded = (top, section_permute(right[cut:], [(last - 1, 1)]))
        pieces[i] = (hidden, left, right) + forwarded
    pieces[-1] = (finished,) + pieces[-1][1:]
    embedded, squares = run_embed(places, pieces, proj_gain_row, proj_weight, text_squares)
    others = [
        section_permute(squares, [(i, (i + by) % SECTIONS) for i in range(SECTIONS)])
        for by in range(1, SECTIONS)
    ]
    out = run_place(
        positions, counts, text_rows[0], embedded, llm_gain_row, [squares] + others, patches
    )
    return out[None]


def solution(mesh):
    in_specs = (
        P("dp", None, None, None),
        P("dp", None),
        P("dp", None),
        P("dp", None, "section"),
        P("section", None),
        P("section", "dp", None),
        P("section", "dp", None),
        P(),
        P(None, "section"),
        P("section"),
    )
    out_specs = P("dp", None, "section")
    return jax.shard_map(
        on_device, mesh=mesh, in_specs=in_specs, out_specs=out_specs, check_vma=False
    )
```

```python
import functools

import jax
import jax.numpy as jnp
from jax import lax
from jax.experimental import pallas as pl
from jax.experimental.pallas import tpu as pltpu
from jax.sharding import PartitionSpec as P

HEAD = 128
LV = 4096
SECTIONS = 4
NY, NZ, NX, NC = 4, 2, 4, 2


def dp_index(y, z, x, c):
    return ((y * NZ + z) * NX + x) * NC + c


def dp_permute(array, dy=0, dz=0, dx=0, dc=0):
    pairs = []
    for y in range(NY):
        for z in range(NZ):
            for x in range(NX):
                for c in range(NC):
                    target = dp_index((y + dy) % NY, (z + dz) % NZ, (x + dx) % NX, (c + dc) % NC)
                    pairs.append((dp_index(y, z, x, c), target))
    return lax.ppermute(array, "dp", pairs)


def ring(block, axis, first, second):
    before = dp_permute(block, **{axis: 1})
    after = dp_permute(block, **{axis: -1})
    onward = before[first], after[second]
    far_first = dp_permute(onward[0], **{axis: 1})
    far_second = dp_permute(onward[1], **{axis: -1})
    return (block, after, before, far_first, far_second), onward


def line_kernel(places, *refs):
    blocks, lines, sems = refs[:10], refs[10:12], refs[12]
    made = []
    for which in range(2):
        own, after, before, far_first, far_second = blocks[which * 5 : which * 5 + 5]
        cut = far_first.shape[1]
        plan = [(own, 0, None), (after, 1, None), (before, 3, None)]
        plan += [(far_first, 2, pl.ds(0, cut)), (far_second, 2, pl.ds(cut, far_second.shape[1]))]
        for at, (block, by, columns) in enumerate(plan):
            target = lines[which].at[lax.rem(places[1 + which] + by, 4)]
            if columns is not None:
                target = target.at[:, columns]
            made.append(pltpu.make_async_copy(block, target, sems.at[which, at]))
    for copy in made:
        copy.start()
    for copy in made:
        copy.wait()


def gather_lines(block_a, block_b, places):
    cut = block_a.shape[1] // HEAD // 2 * HEAD
    parts = ((slice(None), slice(0, cut)), (slice(None), slice(cut, None)))
    blocks = ring(block_a, "dx", *parts)[0] + ring(block_b, "dy", *parts)[0]
    shape = jax.ShapeDtypeStruct((4,) + block_a.shape, block_a.dtype)
    lines = pl.pallas_call(
        line_kernel,
        out_shape=(shape, shape),
        in_specs=[pl.BlockSpec(memory_space=pltpu.SMEM)] + [pl.BlockSpec(memory_space=pl.ANY)] * 10,
        out_specs=(pl.BlockSpec(memory_space=pl.ANY),) * 2,
        scratch_shapes=[pltpu.SemaphoreType.DMA((2, 5))],
        compiler_params=pltpu.CompilerParams(vmem_limit_bytes=1024 * 1024),
        name="lines",
    )(places, *blocks)
    return tuple(line.reshape(-1, line.shape[2]) for line in lines)


def section_permute(array, pairs):
    return lax.ppermute(array, "section", pairs)


def reorder(values, order):
    size = values.shape[1] // (NY * NZ * NX)
    starts = []
    if order == "a":
        for y in range(NY):
            for x in range(NX):
                for z in range(NZ):
                    starts.append(((y * NZ + z) * NX + x) * size)
    else:
        for x in range(NX):
            for y in range(NY):
                for z in range(NZ):
                    starts.append(((y * NZ + z) * NX + x) * size)
    return jnp.concatenate([values[:, s : s + size] for s in starts], 1)


def weights_kernel(plan, sides, places, *refs):
    weights, sems = refs[-2], refs[-1]
    sources = list(refs[: len(sides) * 2 * len(plan)])
    if len(sources[0].shape) == 3:
        sources = [sources[0].at[i] for i in range(sources[0].shape[0])] + list(refs[1:])
    core = places[0]
    line = weights.shape[1] // 4
    made = []
    for at, side in enumerate(sides):
        for which in range(2):
            matrix = 2 * lax.rem(core + side, 2) + which
            for by, skip, rows in plan:
                start = pl.multiple_of(lax.rem(places[2 - which] + by, 4) * line + skip, 16)
                target = weights.at[matrix, pl.ds(start, rows)]
                made.append(pltpu.make_async_copy(sources[len(made)], target, sems.at[len(made)]))
    for copy in made:
        copy.start()
    for copy in made:
        copy.wait()


def hold_weights(blocks, plan, sides, places, held=None):
    width = blocks[0].shape[-1]
    anywhere = pl.BlockSpec(memory_space=pl.ANY)
    vmem = pl.BlockSpec(memory_space=pltpu.VMEM)
    more = () if held is None else (pltpu.with_memory_space_constraint(held, pltpu.VMEM),)
    return pl.pallas_call(
        functools.partial(weights_kernel, plan, sides),
        out_shape=pltpu.VMEM((4, width, width), jnp.bfloat16),
        in_specs=[pl.BlockSpec(memory_space=pltpu.SMEM)]
        + [anywhere] * len(blocks)
        + [vmem] * len(more),
        out_specs=vmem,
        input_output_aliases={1 + len(blocks): 0} if more else {},
        scratch_shapes=[pltpu.SemaphoreType.DMA((len(sides) * 2 * len(plan),))],
        compiler_params=pltpu.CompilerParams(vmem_limit_bytes=1024 * 1024),
        cost_estimate=pl.CostEstimate(flops=0, bytes_accessed=width, transcendentals=0),
        name="weights",
    )(places, *blocks, *more)


def stack_kernel(*refs):
    blocks, out, sems = refs[:-2], refs[-2], refs[-1]
    made = [
        pltpu.make_async_copy(block, out.at[i], sems.at[i]) for i, block in enumerate(blocks)
    ]
    for copy in made:
        copy.start()
    for copy in made:
        copy.wait()


def stack(blocks):
    return pl.pallas_call(
        stack_kernel,
        out_shape=jax.ShapeDtypeStruct((len(blocks),) + blocks[0].shape, blocks[0].dtype),
        in_specs=[pl.BlockSpec(memory_space=pl.ANY)] * len(blocks),
        out_specs=pl.BlockSpec(memory_space=pl.ANY),
        scratch_shapes=[pltpu.SemaphoreType.DMA((len(blocks),))],
        compiler_params=pltpu.CompilerParams(vmem_limit_bytes=1024 * 1024),
        cost_estimate=pl.CostEstimate(flops=0, bytes_accessed=1024, transcendentals=0),
        name="stack",
    )(*blocks)


def first_layer_kernel(patches, places, hidden, gain, weights, out, mixed):
    @pl.when(places[3] == 0)
    def _():
        layer_kernel(patches, hidden, gain, weights, out, mixed)

    @pl.when(places[3] != 0)
    def _():
        out[...] = jnp.zeros_like(out)


def layer_kernel(patches, hidden, gain, weights, out, mixed):
    rows, width = hidden.shape
    heads = width // HEAD
    widened = hidden[...].astype(jnp.float32)
    normed = widened * lax.rsqrt(jnp.mean(widened * widened, -1, keepdims=True) + 1e-06)
    normed = (normed * gain[...].astype(jnp.float32)).astype(jnp.bfloat16)
    normed_a, normed_b = reorder(normed, "a"), reorder(normed, "b")
    tiles = [(at, min(256, width - at)) for at in range(0, width, 256)]

    def dot(left, right):
        return jnp.dot(left, right, preferred_element_type=jnp.float32)

    query, key, value = [], [], []
    for at, size in tiles:
        for matrix, left, parts in ((0, normed_a, query), (1, normed_b, key), (2, normed_a, value)):
            product = dot(left, weights[matrix, :, at : at + size]).astype(jnp.bfloat16)
            parts.extend(product[:, i : i + HEAD] for i in range(0, size, HEAD))
    scores = jnp.stack(
        [
            lax.dot_general(q, k, (((1,), (1,)), ((), ())), preferred_element_type=jnp.float32)
            for q, k in zip(query, key)
        ]
    ) * HEAD ** (-0.5)
    if rows != patches:
        row_image = lax.broadcasted_iota(jnp.int32, (rows, rows), 0) // patches
        column_image = lax.broadcasted_iota(jnp.int32, (rows, rows), 1) // patches
        scores = jnp.where((row_image == column_image)[None], scores, -jnp.inf)
    raised = jnp.exp(scores - jnp.max(scores, -1, keepdims=True))
    shares = (raised / jnp.sum(raised, -1, keepdims=True)).astype(jnp.bfloat16)
    for head in range(heads):
        mixed[:, head * HEAD : head * HEAD + HEAD] = dot(shares[head], value[head]).astype(
            jnp.bfloat16
        )
    mixed_b = reorder(mixed[...], "b")
    for at, size in tiles:
        added = dot(mixed_b, weights[3, :, at : at + size])
        out[:, at : at + size] = (
            hidden[:, at : at + size].astype(jnp.float32) + added
        ).astype(jnp.bfloat16)


def run_layer(stage, places, hidden, gain_row, weights, patches):
    rows, width = hidden.shape
    vmem = pl.BlockSpec(memory_space=pltpu.VMEM)
    weights = pltpu.with_memory_space_constraint(weights, pltpu.VMEM)
    kernel = first_layer_kernel if stage == 0 else layer_kernel
    scalars = (places,) if stage == 0 else ()
    return pl.pallas_call(
        functools.partial(kernel, patches),
        out_shape=jax.ShapeDtypeStruct((rows, width), jnp.bfloat16),
        in_specs=[pl.BlockSpec(memory_space=pltpu.SMEM)] * len(scalars) + [vmem] * 3,
        out_specs=vmem,
        scratch_shapes=[pltpu.VMEM((rows, width), jnp.bfloat16)],
        compiler_params=pltpu.CompilerParams(vmem_limit_bytes=12 * 1024 * 1024),
        cost_estimate=pl.CostEstimate(
            flops=8 * rows * width * width,
            bytes_accessed=4 * rows * width,
            transcendentals=rows * rows * width // HEAD,
        ),
        name="layer",
    )(*scalars, hidden, gain_row, weights)


def diagonal(size):
    row = lax.broadcasted_iota(jnp.int32, (size, size), 0)
    return row == lax.broadcasted_iota(jnp.int32, (size, size), 1)


def embed_kernel(spans, places, gain, weight, text_squares, *refs):
    parts, (embedded, squares) = refs[:-2], refs[-2:]
    rows, columns = embedded.shape
    values = []
    for first, count in spans:
        own, left, right, *forwarded = (part[...] for part in parts[first : first + count])
        halves = jnp.concatenate(forwarded, 0)
        total = jnp.where(places[3] == 0, left, jnp.where(places[3] == 1, halves, right))
        values.append(jnp.where(places[3] == SECTIONS - 1, own, total).astype(jnp.float32))
    values = jnp.concatenate(values, 0)
    centered = values - jnp.mean(values, -1, keepdims=True)
    variance = jnp.mean(centered * centered, -1, keepdims=True)
    normed = centered * lax.rsqrt(variance + 1e-05) * gain[...].astype(jnp.float32)
    normed = normed.astype(jnp.bfloat16)
    total = jnp.zeros((rows, 1), jnp.float32)
    for at in range(0, columns, 256):
        projected = jnp.dot(
            normed, weight[:, at : at + 256], preferred_element_type=jnp.float32
        )
        part = (0.5 * projected * (1.0 + lax.erf(projected * 0.5**0.5))).astype(jnp.bfloat16)
        embedded[:, at : at + 256] = part
        part = part.astype(jnp.float32)
        total = total + jnp.sum(part * part, -1, keepdims=True)
    squares[:, :rows] = jnp.sum(jnp.where(diagonal(rows), total, 0.0), 0, keepdims=True)
    squares[:, rows:] = text_squares[...]


def run_embed(places, pieces, gain_row, weight, text_squares):
    rows, columns = sum(piece[0].shape[0] for piece in pieces), weight.shape[1]
    parts = sum(pieces, ())
    firsts = [sum(len(piece) for piece in pieces[:i]) for i in range(len(pieces))]
    spans = [(first, len(piece)) for first, piece in zip(firsts, pieces)]
    vmem = pl.BlockSpec(memory_space=pltpu.VMEM)
    return pl.pallas_call(
        functools.partial(embed_kernel, spans),
        out_shape=(
            jax.ShapeDtypeStruct((rows, columns), jnp.bfloat16),
            jax.ShapeDtypeStruct((1, rows + text_squares.shape[1]), jnp.float32),
        ),
        in_specs=[pl.BlockSpec(memory_space=pltpu.SMEM)] + [vmem] * (3 + len(parts)),
        out_specs=(vmem, vmem),
        compiler_params=pltpu.CompilerParams(vmem_limit_bytes=12 * 1024 * 1024),
        name="embed",
    )(places, gain_row, weight, text_squares, *parts)


def place_kernel(patches, positions, counts, text, embedded, gain, *refs):
    squares, out = refs[:-1], refs[-1]
    length = text.shape[0]
    rows = embedded.shape[0]
    total = squares[0][...]
    for part in squares[1:]:
        total = total + part[...]
    scales = lax.rsqrt(total / LV + 1e-06)
    columns = []
    for first in range(0, scales.shape[1], rows):
        part = jnp.where(diagonal(rows), scales[:, first : first + rows], 0.0)
        columns.append(jnp.sum(part, 1, keepdims=True))
    gain_row = gain[...].astype(jnp.float32)

    def scale(values, column):
        return (values.astype(jnp.float32) * column * gain_row).astype(jnp.bfloat16)

    scaled = scale(embedded[...], columns[0])
    at = lax.broadcasted_iota(jnp.int32, (length, patches), 0)
    patch = lax.broadcasted_iota(jnp.int32, (length, patches), 1)
    one_row = lax.broadcasted_iota(jnp.int32, (length, 1), 0)
    picks, taken = [], None
    for slot in range(rows // patches):
        start, here = positions[0, slot], counts[0, slot] == 1
        picks.append(jnp.where((at == patch + start) & here, 1.0, 0.0).astype(jnp.bfloat16))
        inside = (one_row >= start) & (one_row < start + patches) & here
        taken = inside if taken is None else taken | inside
    placed = jnp.dot(
        jnp.concatenate(picks, 1), scaled, preferred_element_type=jnp.float32
    ).astype(jnp.bfloat16)
    out[...] = jnp.where(taken, placed, scale(text[...], jnp.concatenate(columns[1:], 0)))


def run_place(positions, counts, text, embedded, gain_row, squares, patches):
    vmem = pl.BlockSpec(memory_space=pltpu.VMEM)
    smem = pl.BlockSpec(memory_space=pltpu.SMEM)
    return pl.pallas_call(
        functools.partial(place_kernel, patches),
        out_shape=jax.ShapeDtypeStruct(text.shape, jnp.bfloat16),
        in_specs=[smem, smem] + [vmem] * (3 + len(squares)),
        out_specs=vmem,
        compiler_params=pltpu.CompilerParams(vmem_limit_bytes=12 * 1024 * 1024),
        name="place",
    )(positions, counts, text, embedded, gain_row, *squares)


def on_device(
    images, counts, positions, text_rows, norm_gain, w_qkv, w_out, proj_gain, proj_weight, llm_gain
):
    section = lax.axis_index("section")
    place = lax.axis_index("dp")
    core = place % NC
    x_place = (place // NC) % NX
    z_place = (place // (NC * NX)) % NZ
    y_place = place // (NC * NX * NZ)
    width = w_out.shape[2]
    micro, patches = images.shape[1], images.shape[2]

    places = jnp.stack([core, x_place, y_place, section]).astype(jnp.int32)

    text = text_rows[0].astype(jnp.float32)
    text_squares = jnp.sum(text * text, -1)[None]

    is_first = core == 0
    is_low = z_place == 0
    parts = [w_qkv[0][:, i * width : (i + 1) * width] for i in range(3)] + [w_out[0]]
    keep = jnp.concatenate([jnp.where(is_first, parts[i], parts[i + 2]) for i in (0, 1)], 1)
    give = jnp.concatenate([jnp.where(is_first, parts[i + 2], parts[i]) for i in (0, 1)], 1)
    got = dp_permute(give, dc=1)
    pair = jnp.concatenate([jnp.where(is_first, keep, got), jnp.where(is_first, got, keep)], 0)
    other = dp_permute(pair, dz=1)
    quad = jnp.concatenate([jnp.where(is_low, pair, other), jnp.where(is_low, other, pair)], 0)
    line_a, line_b = gather_lines(quad[:, :width], quad[:, width:], places)
    half = line_a.shape[0] // 2
    top, low = slice(0, half), slice(half, None)
    mine_a, onward_a = ring(line_a, "dy", top, low)
    mine_b, onward_b = ring(line_b, "dx", top, low)
    mine = (mine_a, mine_b)
    early = [images[0, i] for i in range(micro)]
    early += [norm_gain[0].reshape(1, width), proj_gain.reshape(1, width), llm_gain.reshape(1, -1)]
    places, text_squares, *early = lax.optimization_barrier((places, text_squares, *early))
    pieces, (gain_row, proj_gain_row, llm_gain_row) = early[:micro], early[micro:]
    near = sum((part[:3] for part in mine), ())
    near = lax.optimization_barrier((near, onward_a, onward_b))[0]
    line = line_a.shape[0]
    plan = ((0, 0, line), (1, 0, line), (3, 0, line))
    swapped = dp_permute(stack(near), dc=1)
    weights = hold_weights((swapped,) + near, plan, (1, 0), places)
    far = sum((part[3:] for part in mine), ())
    far = far + tuple(dp_permute(part, dc=1) for part in far)
    weights = hold_weights(far, ((2, 0, half), (2, half, half)), (0, 1), places, weights)

    last = SECTIONS - 1
    for stage in range(SECTIONS):
        moved = []
        for hidden in pieces:
            hidden = run_layer(stage, places, hidden, gain_row, weights, patches)
            if stage < last:
                moved.append(section_permute(hidden, [(stage, stage + 1)]))
            else:
                left = section_permute(hidden, [(last, 0)])
                right = section_permute(hidden, [(last, last - 1)])
                moved.append((hidden, left, right))
        pieces = moved
    finished = pieces[-1][0]
    for i, (hidden, left, right) in enumerate(pieces):
        left, right, finished = lax.optimization_barrier((left, right, finished))
        if i + 1 < micro:
            forwarded = (section_permute(right, [(last - 1, 1)]),)
        else:
            cut = hidden.shape[0] // 4
            top = section_permute(left[:cut], [(0, 1)])
            forwarded = (top, section_permute(right[cut:], [(last - 1, 1)]))
        pieces[i] = (hidden, left, right) + forwarded
    pieces[-1] = (finished,) + pieces[-1][1:]
    embedded, squares = run_embed(places, pieces, proj_gain_row, proj_weight, text_squares)
    others = [
        section_permute(squares, [(i, (i + by) % SECTIONS) for i in range(SECTIONS)])
        for by in range(1, SECTIONS)
    ]
    out = run_place(
        positions, counts, text_rows[0], embedded, llm_gain_row, [squares] + others, patches
    )
    return out[None]


def solution(mesh):
    in_specs = (
        P("dp", None, None, None),
        P("dp", None),
        P("dp", None),
        P("dp", None, "section"),
        P("section", None),
        P("section", "dp", None),
        P("section", "dp", None),
        P(),
        P(None, "section"),
        P("section"),
    )
    out_specs = P("dp", None, "section")
    return jax.shard_map(
        on_device, mesh=mesh, in_specs=in_specs, out_specs=out_specs, check_vma=False
    )
```

```python
import functools

import jax
import jax.numpy as jnp
from jax import lax
from jax.experimental import pallas as pl
from jax.experimental.pallas import tpu as pltpu
from jax.sharding import PartitionSpec as P

HEAD = 128
LV = 4096
SECTIONS = 4
NY, NZ, NX, NC = 4, 2, 4, 2


def dp_index(y, z, x, c):
    return ((y * NZ + z) * NX + x) * NC + c


def dp_permute(array, dy=0, dz=0, dx=0, dc=0):
    pairs = []
    for y in range(NY):
        for z in range(NZ):
            for x in range(NX):
                for c in range(NC):
                    target = dp_index((y + dy) % NY, (z + dz) % NZ, (x + dx) % NX, (c + dc) % NC)
                    pairs.append((dp_index(y, z, x, c), target))
    return lax.ppermute(array, "dp", pairs)


def ring(block, axis, first, second):
    before = dp_permute(block, **{axis: 1})
    after = dp_permute(block, **{axis: -1})
    onward = before[first], after[second]
    far_first = dp_permute(onward[0], **{axis: 1})
    far_second = dp_permute(onward[1], **{axis: -1})
    return (block, after, before, far_first, far_second), onward


def line_kernel(places, *refs):
    blocks, lines, sems = refs[:10], refs[10:12], refs[12]
    made = []
    for which in range(2):
        own, after, before, far_first, far_second = blocks[which * 5 : which * 5 + 5]
        cut = far_first.shape[1]
        plan = [(own, 0, None), (after, 1, None), (before, 3, None)]
        plan += [(far_first, 2, pl.ds(0, cut)), (far_second, 2, pl.ds(cut, far_second.shape[1]))]
        for at, (block, by, columns) in enumerate(plan):
            target = lines[which].at[lax.rem(places[1 + which] + by, 4)]
            if columns is not None:
                target = target.at[:, columns]
            made.append(pltpu.make_async_copy(block, target, sems.at[which, at]))
    for copy in made:
        copy.start()
    for copy in made:
        copy.wait()


def gather_lines(block_a, block_b, places):
    cut = block_a.shape[1] // HEAD // 2 * HEAD
    parts = ((slice(None), slice(0, cut)), (slice(None), slice(cut, None)))
    blocks = ring(block_a, "dx", *parts)[0] + ring(block_b, "dy", *parts)[0]
    shape = jax.ShapeDtypeStruct((4,) + block_a.shape, block_a.dtype)
    lines = pl.pallas_call(
        line_kernel,
        out_shape=(shape, shape),
        in_specs=[pl.BlockSpec(memory_space=pltpu.SMEM)] + [pl.BlockSpec(memory_space=pl.ANY)] * 10,
        out_specs=(pl.BlockSpec(memory_space=pl.ANY),) * 2,
        scratch_shapes=[pltpu.SemaphoreType.DMA((2, 5))],
        compiler_params=pltpu.CompilerParams(vmem_limit_bytes=1024 * 1024),
        name="lines",
    )(places, *blocks)
    return tuple(line.reshape(-1, line.shape[2]) for line in lines)


def section_permute(array, pairs):
    return lax.ppermute(array, "section", pairs)


def reorder(values, order):
    size = values.shape[1] // (NY * NZ * NX)
    starts = []
    if order == "a":
        for y in range(NY):
            for x in range(NX):
                for z in range(NZ):
                    starts.append(((y * NZ + z) * NX + x) * size)
    else:
        for x in range(NX):
            for y in range(NY):
                for z in range(NZ):
                    starts.append(((y * NZ + z) * NX + x) * size)
    return jnp.concatenate([values[:, s : s + size] for s in starts], 1)


def weights_kernel(plans, sides, places, *refs):
    weights, sems = refs[-2], refs[-1]
    sources = list(refs)
    if len(sources[0].shape) == 3:
        sources = [refs[0].at[i] for i in range(refs[0].shape[0])] + list(refs[1:])
    core = places[0]
    line = weights.shape[1] // 4
    made = []
    for side, plan in zip(sides, plans):
        for which in range(2):
            matrix = 2 * lax.rem(core + side, 2) + which
            for by, skip, rows in plan:
                start = pl.multiple_of(lax.rem(places[2 - which] + by, 4) * line + skip, 16)
                target = weights.at[matrix, pl.ds(start, rows)]
                made.append(pltpu.make_async_copy(sources[len(made)], target, sems.at[len(made)]))
    for copy in made:
        copy.start()
    for copy in made:
        copy.wait()


def hold_weights(blocks, plans, sides, places, held=None):
    width = blocks[0].shape[-1]
    anywhere = pl.BlockSpec(memory_space=pl.ANY)
    vmem = pl.BlockSpec(memory_space=pltpu.VMEM)
    more = () if held is None else (pltpu.with_memory_space_constraint(held, pltpu.VMEM),)
    return pl.pallas_call(
        functools.partial(weights_kernel, plans, sides),
        out_shape=pltpu.VMEM((4, width, width), jnp.bfloat16),
        in_specs=[pl.BlockSpec(memory_space=pltpu.SMEM)]
        + [anywhere] * len(blocks)
        + [vmem] * len(more),
        out_specs=vmem,
        input_output_aliases={1 + len(blocks): 0} if more else {},
        scratch_shapes=[pltpu.SemaphoreType.DMA((2 * sum(len(plan) for plan in plans),))],
        compiler_params=pltpu.CompilerParams(vmem_limit_bytes=1024 * 1024),
        cost_estimate=pl.CostEstimate(flops=0, bytes_accessed=width, transcendentals=0),
        name="weights",
    )(places, *blocks, *more)


def stack_kernel(*refs):
    blocks, out, sems = refs[:-2], refs[-2], refs[-1]
    made = [
        pltpu.make_async_copy(block, out.at[i], sems.at[i]) for i, block in enumerate(blocks)
    ]
    for copy in made:
        copy.start()
    for copy in made:
        copy.wait()


def stack(blocks):
    return pl.pallas_call(
        stack_kernel,
        out_shape=jax.ShapeDtypeStruct((len(blocks),) + blocks[0].shape, blocks[0].dtype),
        in_specs=[pl.BlockSpec(memory_space=pl.ANY)] * len(blocks),
        out_specs=pl.BlockSpec(memory_space=pl.ANY),
        scratch_shapes=[pltpu.SemaphoreType.DMA((len(blocks),))],
        compiler_params=pltpu.CompilerParams(vmem_limit_bytes=1024 * 1024),
        cost_estimate=pl.CostEstimate(flops=0, bytes_accessed=1024, transcendentals=0),
        name="stack",
    )(*blocks)


def first_layer_kernel(patches, places, hidden, gain, weights, out, mixed):
    @pl.when(places[3] == 0)
    def _():
        layer_kernel(patches, hidden, gain, weights, out, mixed)

    @pl.when(places[3] != 0)
    def _():
        out[...] = jnp.zeros_like(out)


def layer_kernel(patches, hidden, gain, weights, out, mixed):
    rows, width = hidden.shape
    heads = width // HEAD
    widened = hidden[...].astype(jnp.float32)
    normed = widened * lax.rsqrt(jnp.mean(widened * widened, -1, keepdims=True) + 1e-06)
    normed = (normed * gain[...].astype(jnp.float32)).astype(jnp.bfloat16)
    normed_a, normed_b = reorder(normed, "a"), reorder(normed, "b")
    tiles = [(at, min(256, width - at)) for at in range(0, width, 256)]

    def dot(left, right):
        return jnp.dot(left, right, preferred_element_type=jnp.float32)

    query, key, value = [], [], []
    for at, size in tiles:
        for matrix, left, parts in ((0, normed_a, query), (1, normed_b, key), (2, normed_a, value)):
            product = dot(left, weights[matrix, :, at : at + size]).astype(jnp.bfloat16)
            parts.extend(product[:, i : i + HEAD] for i in range(0, size, HEAD))
    scores = jnp.stack(
        [
            lax.dot_general(q, k, (((1,), (1,)), ((), ())), preferred_element_type=jnp.float32)
            for q, k in zip(query, key)
        ]
    ) * HEAD ** (-0.5)
    if rows != patches:
        row_image = lax.broadcasted_iota(jnp.int32, (rows, rows), 0) // patches
        column_image = lax.broadcasted_iota(jnp.int32, (rows, rows), 1) // patches
        scores = jnp.where((row_image == column_image)[None], scores, -jnp.inf)
    raised = jnp.exp(scores - jnp.max(scores, -1, keepdims=True))
    shares = (raised / jnp.sum(raised, -1, keepdims=True)).astype(jnp.bfloat16)
    for head in range(heads):
        mixed[:, head * HEAD : head * HEAD + HEAD] = dot(shares[head], value[head]).astype(
            jnp.bfloat16
        )
    mixed_b = reorder(mixed[...], "b")
    for at, size in tiles:
        added = dot(mixed_b, weights[3, :, at : at + size])
        out[:, at : at + size] = (
            hidden[:, at : at + size].astype(jnp.float32) + added
        ).astype(jnp.bfloat16)


def run_layer(stage, places, hidden, gain_row, weights, patches):
    rows, width = hidden.shape
    vmem = pl.BlockSpec(memory_space=pltpu.VMEM)
    weights = pltpu.with_memory_space_constraint(weights, pltpu.VMEM)
    kernel = first_layer_kernel if stage == 0 else layer_kernel
    scalars = (places,) if stage == 0 else ()
    return pl.pallas_call(
        functools.partial(kernel, patches),
        out_shape=jax.ShapeDtypeStruct((rows, width), jnp.bfloat16),
        in_specs=[pl.BlockSpec(memory_space=pltpu.SMEM)] * len(scalars) + [vmem] * 3,
        out_specs=vmem,
        scratch_shapes=[pltpu.VMEM((rows, width), jnp.bfloat16)],
        compiler_params=pltpu.CompilerParams(vmem_limit_bytes=12 * 1024 * 1024),
        cost_estimate=pl.CostEstimate(
            flops=8 * rows * width * width,
            bytes_accessed=4 * rows * width,
            transcendentals=rows * rows * width // HEAD,
        ),
        name="layer",
    )(*scalars, hidden, gain_row, weights)


def diagonal(size):
    row = lax.broadcasted_iota(jnp.int32, (size, size), 0)
    return row == lax.broadcasted_iota(jnp.int32, (size, size), 1)


def embed_kernel(spans, places, gain, weight, text_squares, *refs):
    parts, (embedded, squares) = refs[:-2], refs[-2:]
    rows, columns = embedded.shape
    values = []
    for first, count in spans:
        own, left, right, *forwarded = (part[...] for part in parts[first : first + count])
        halves = jnp.concatenate(forwarded, 0)
        total = jnp.where(places[3] == 0, left, jnp.where(places[3] == 1, halves, right))
        values.append(jnp.where(places[3] == SECTIONS - 1, own, total).astype(jnp.float32))
    values = jnp.concatenate(values, 0)
    centered = values - jnp.mean(values, -1, keepdims=True)
    variance = jnp.mean(centered * centered, -1, keepdims=True)
    normed = centered * lax.rsqrt(variance + 1e-05) * gain[...].astype(jnp.float32)
    normed = normed.astype(jnp.bfloat16)
    total = jnp.zeros((rows, 1), jnp.float32)
    for at in range(0, columns, 256):
        projected = jnp.dot(
            normed, weight[:, at : at + 256], preferred_element_type=jnp.float32
        )
        part = (0.5 * projected * (1.0 + lax.erf(projected * 0.5**0.5))).astype(jnp.bfloat16)
        embedded[:, at : at + 256] = part
        part = part.astype(jnp.float32)
        total = total + jnp.sum(part * part, -1, keepdims=True)
    squares[:, :rows] = jnp.sum(jnp.where(diagonal(rows), total, 0.0), 0, keepdims=True)
    squares[:, rows:] = text_squares[...]


def run_embed(places, pieces, gain_row, weight, text_squares):
    rows, columns = sum(piece[0].shape[0] for piece in pieces), weight.shape[1]
    parts = sum(pieces, ())
    firsts = [sum(len(piece) for piece in pieces[:i]) for i in range(len(pieces))]
    spans = [(first, len(piece)) for first, piece in zip(firsts, pieces)]
    vmem = pl.BlockSpec(memory_space=pltpu.VMEM)
    return pl.pallas_call(
        functools.partial(embed_kernel, spans),
        out_shape=(
            jax.ShapeDtypeStruct((rows, columns), jnp.bfloat16),
            jax.ShapeDtypeStruct((1, rows + text_squares.shape[1]), jnp.float32),
        ),
        in_specs=[pl.BlockSpec(memory_space=pltpu.SMEM)] + [vmem] * (3 + len(parts)),
        out_specs=(vmem, vmem),
        compiler_params=pltpu.CompilerParams(vmem_limit_bytes=12 * 1024 * 1024),
        name="embed",
    )(places, gain_row, weight, text_squares, *parts)


def place_kernel(patches, positions, counts, text, embedded, gain, *refs):
    squares, out = refs[:-1], refs[-1]
    length = text.shape[0]
    rows = embedded.shape[0]
    total = squares[0][...]
    for part in squares[1:]:
        total = total + part[...]
    scales = lax.rsqrt(total / LV + 1e-06)
    columns = []
    for first in range(0, scales.shape[1], rows):
        part = jnp.where(diagonal(rows), scales[:, first : first + rows], 0.0)
        columns.append(jnp.sum(part, 1, keepdims=True))
    gain_row = gain[...].astype(jnp.float32)

    def scale(values, column):
        return (values.astype(jnp.float32) * column * gain_row).astype(jnp.bfloat16)

    scaled = scale(embedded[...], columns[0])
    at = lax.broadcasted_iota(jnp.int32, (length, patches), 0)
    patch = lax.broadcasted_iota(jnp.int32, (length, patches), 1)
    one_row = lax.broadcasted_iota(jnp.int32, (length, 1), 0)
    picks, taken = [], None
    for slot in range(rows // patches):
        start, here = positions[0, slot], counts[0, slot] == 1
        picks.append(jnp.where((at == patch + start) & here, 1.0, 0.0).astype(jnp.bfloat16))
        inside = (one_row >= start) & (one_row < start + patches) & here
        taken = inside if taken is None else taken | inside
    placed = jnp.dot(
        jnp.concatenate(picks, 1), scaled, preferred_element_type=jnp.float32
    ).astype(jnp.bfloat16)
    out[...] = jnp.where(taken, placed, scale(text[...], jnp.concatenate(columns[1:], 0)))


def run_place(positions, counts, text, embedded, gain_row, squares, patches):
    vmem = pl.BlockSpec(memory_space=pltpu.VMEM)
    smem = pl.BlockSpec(memory_space=pltpu.SMEM)
    return pl.pallas_call(
        functools.partial(place_kernel, patches),
        out_shape=jax.ShapeDtypeStruct(text.shape, jnp.bfloat16),
        in_specs=[smem, smem] + [vmem] * (3 + len(squares)),
        out_specs=vmem,
        compiler_params=pltpu.CompilerParams(vmem_limit_bytes=12 * 1024 * 1024),
        name="place",
    )(positions, counts, text, embedded, gain_row, *squares)


def on_device(
    images, counts, positions, text_rows, norm_gain, w_qkv, w_out, proj_gain, proj_weight, llm_gain
):
    section = lax.axis_index("section")
    place = lax.axis_index("dp")
    core = place % NC
    x_place = (place // NC) % NX
    z_place = (place // (NC * NX)) % NZ
    y_place = place // (NC * NX * NZ)
    width = w_out.shape[2]
    micro, patches = images.shape[1], images.shape[2]

    places = jnp.stack([core, x_place, y_place, section]).astype(jnp.int32)

    text = text_rows[0].astype(jnp.float32)
    text_squares = jnp.sum(text * text, -1)[None]

    is_first = core == 0
    is_low = z_place == 0
    parts = [w_qkv[0][:, i * width : (i + 1) * width] for i in range(3)] + [w_out[0]]
    keep = jnp.concatenate([jnp.where(is_first, parts[i], parts[i + 2]) for i in (0, 1)], 1)
    give = jnp.concatenate([jnp.where(is_first, parts[i + 2], parts[i]) for i in (0, 1)], 1)
    got = dp_permute(give, dc=1)
    pair = jnp.concatenate([jnp.where(is_first, keep, got), jnp.where(is_first, got, keep)], 0)
    other = dp_permute(pair, dz=1)
    quad = jnp.concatenate([jnp.where(is_low, pair, other), jnp.where(is_low, other, pair)], 0)
    line_a, line_b = gather_lines(quad[:, :width], quad[:, width:], places)
    half = line_a.shape[0] // 2
    top, low = slice(0, half), slice(half, None)
    mine_a, onward_a = ring(line_a, "dy", top, low)
    mine_b, onward_b = ring(line_b, "dx", top, low)
    mine = (mine_a, mine_b)
    early = [images[0, i] for i in range(micro)]
    early += [norm_gain[0].reshape(1, width), proj_gain.reshape(1, width), llm_gain.reshape(1, -1)]
    places, text_squares, *early = lax.optimization_barrier((places, text_squares, *early))
    pieces, (gain_row, proj_gain_row, llm_gain_row) = early[:micro], early[micro:]
    near = sum((part[:3] for part in mine), ())
    near = lax.optimization_barrier((near, onward_a, onward_b))[0]
    line = line_a.shape[0]
    plan = ((0, 0, line), (1, 0, line), (3, 0, line))
    swapped = dp_permute(stack(near), dc=1)
    far_plan = ((2, 0, half), (2, half, half))
    own = sum((near[i * 3 : i * 3 + 3] + mine[i][3:] for i in (0, 1)), ())
    weights = hold_weights((swapped,) + own, (plan, plan + far_plan), (1, 0), places)
    far = tuple(dp_permute(part, dc=1) for part in mine[0][3:] + mine[1][3:])
    weights = hold_weights(far, (far_plan,), (1,), places, weights)

    last = SECTIONS - 1
    for stage in range(SECTIONS):
        moved = []
        for hidden in pieces:
            hidden = run_layer(stage, places, hidden, gain_row, weights, patches)
            if stage < last:
                moved.append(section_permute(hidden, [(stage, stage + 1)]))
            else:
                left = section_permute(hidden, [(last, 0)])
                right = section_permute(hidden, [(last, last - 1)])
                moved.append((hidden, left, right))
        pieces = moved
    finished = pieces[-1][0]
    for i, (hidden, left, right) in enumerate(pieces):
        left, right, finished = lax.optimization_barrier((left, right, finished))
        if i + 1 < micro:
            forwarded = (section_permute(right, [(last - 1, 1)]),)
        else:
            cut = hidden.shape[0] // 4
            top = section_permute(left[:cut], [(0, 1)])
            forwarded = (top, section_permute(right[cut:], [(last - 1, 1)]))
        pieces[i] = (hidden, left, right) + forwarded
    pieces[-1] = (finished,) + pieces[-1][1:]
    embedded, squares = run_embed(places, pieces, proj_gain_row, proj_weight, text_squares)
    others = [
        section_permute(squares, [(i, (i + by) % SECTIONS) for i in range(SECTIONS)])
        for by in range(1, SECTIONS)
    ]
    out = run_place(
        positions, counts, text_rows[0], embedded, llm_gain_row, [squares] + others, patches
    )
    return out[None]


def solution(mesh):
    in_specs = (
        P("dp", None, None, None),
        P("dp", None),
        P("dp", None),
        P("dp", None, "section"),
        P("section", None),
        P("section", "dp", None),
        P("section", "dp", None),
        P(),
        P(None, "section"),
        P("section"),
    )
    out_specs = P("dp", None, "section")
    return jax.shard_map(
        on_device, mesh=mesh, in_specs=in_specs, out_specs=out_specs, check_vma=False
    )
```

```python
import functools

import jax
import jax.numpy as jnp
from jax import lax
from jax.experimental import pallas as pl
from jax.experimental.pallas import tpu as pltpu
from jax.sharding import PartitionSpec as P

HEAD = 128
LV = 4096
SECTIONS = 4
NY, NZ, NX, NC = 4, 2, 4, 2


def dp_index(y, z, x, c):
    return ((y * NZ + z) * NX + x) * NC + c


def dp_permute(array, dy=0, dz=0, dx=0, dc=0):
    pairs = []
    for y in range(NY):
        for z in range(NZ):
            for x in range(NX):
                for c in range(NC):
                    target = dp_index((y + dy) % NY, (z + dz) % NZ, (x + dx) % NX, (c + dc) % NC)
                    pairs.append((dp_index(y, z, x, c), target))
    return lax.ppermute(array, "dp", pairs)


def ring(block, axis, first, second):
    before = dp_permute(block, **{axis: 1})
    after = dp_permute(block, **{axis: -1})
    onward = before[first], after[second]
    far_first = dp_permute(onward[0], **{axis: 1})
    far_second = dp_permute(onward[1], **{axis: -1})
    return (block, after, before, far_first, far_second), onward


def line_kernel(places, *refs):
    blocks, lines, sems = refs[:10], refs[10:12], refs[12]
    made = []
    for which in range(2):
        own, after, before, far_first, far_second = blocks[which * 5 : which * 5 + 5]
        cut = far_first.shape[1]
        plan = [(own, 0, None), (after, 1, None), (before, 3, None)]
        plan += [(far_first, 2, pl.ds(0, cut)), (far_second, 2, pl.ds(cut, far_second.shape[1]))]
        for at, (block, by, columns) in enumerate(plan):
            target = lines[which].at[lax.rem(places[1 + which] + by, 4)]
            if columns is not None:
                target = target.at[:, columns]
            made.append(pltpu.make_async_copy(block, target, sems.at[which, at]))
    for copy in made:
        copy.start()
    for copy in made:
        copy.wait()


def gather_lines(block_a, block_b, places):
    cut = block_a.shape[1] // HEAD // 2 * HEAD
    parts = ((slice(None), slice(0, cut)), (slice(None), slice(cut, None)))
    blocks = ring(block_a, "dx", *parts)[0] + ring(block_b, "dy", *parts)[0]
    shape = jax.ShapeDtypeStruct((4,) + block_a.shape, block_a.dtype)
    lines = pl.pallas_call(
        line_kernel,
        out_shape=(shape, shape),
        in_specs=[pl.BlockSpec(memory_space=pltpu.SMEM)] + [pl.BlockSpec(memory_space=pl.ANY)] * 10,
        out_specs=(pl.BlockSpec(memory_space=pl.ANY),) * 2,
        scratch_shapes=[pltpu.SemaphoreType.DMA((2, 5))],
        compiler_params=pltpu.CompilerParams(vmem_limit_bytes=1024 * 1024),
        name="lines",
    )(places, *blocks)
    return tuple(line.reshape(-1, line.shape[2]) for line in lines)


def section_permute(array, pairs):
    return lax.ppermute(array, "section", pairs)


def reorder(values, order):
    size = values.shape[1] // (NY * NZ * NX)
    starts = []
    if order == "a":
        for y in range(NY):
            for x in range(NX):
                for z in range(NZ):
                    starts.append(((y * NZ + z) * NX + x) * size)
    else:
        for x in range(NX):
            for y in range(NY):
                for z in range(NZ):
                    starts.append(((y * NZ + z) * NX + x) * size)
    return jnp.concatenate([values[:, s : s + size] for s in starts], 1)


def weights_kernel(plan, sides, places, *refs):
    weights, sems = refs[-2], refs[-1]
    sources = list(refs[: len(sides) * 2 * len(plan)])
    if len(sources[0].shape) == 3:
        sources = [sources[0].at[i] for i in range(sources[0].shape[0])] + list(refs[1:])
    core = places[0]
    line = weights.shape[1] // 4
    made = []
    for at, side in enumerate(sides):
        for which in range(2):
            matrix = 2 * lax.rem(core + side, 2) + which
            for by, skip, rows in plan:
                start = pl.multiple_of(lax.rem(places[2 - which] + by, 4) * line + skip, 16)
                target = weights.at[matrix, pl.ds(start, rows)]
                made.append(pltpu.make_async_copy(sources[len(made)], target, sems.at[len(made)]))
    for copy in made:
        copy.start()
    for copy in made:
        copy.wait()


def hold_weights(blocks, plan, sides, places, held=None):
    width = blocks[0].shape[-1]
    anywhere = pl.BlockSpec(memory_space=pl.ANY)
    vmem = pl.BlockSpec(memory_space=pltpu.VMEM)
    more = () if held is None else (pltpu.with_memory_space_constraint(held, pltpu.VMEM),)
    return pl.pallas_call(
        functools.partial(weights_kernel, plan, sides),
        out_shape=pltpu.VMEM((4, width, width), jnp.bfloat16),
        in_specs=[pl.BlockSpec(memory_space=pltpu.SMEM)]
        + [anywhere] * len(blocks)
        + [vmem] * len(more),
        out_specs=vmem,
        input_output_aliases={1 + len(blocks): 0} if more else {},
        scratch_shapes=[pltpu.SemaphoreType.DMA((len(sides) * 2 * len(plan),))],
        compiler_params=pltpu.CompilerParams(vmem_limit_bytes=1024 * 1024),
        cost_estimate=pl.CostEstimate(flops=0, bytes_accessed=width, transcendentals=0),
        name="weights",
    )(places, *blocks, *more)


def stack_kernel(*refs):
    blocks, out, sems = refs[:-2], refs[-2], refs[-1]
    made = [
        pltpu.make_async_copy(block, out.at[i], sems.at[i]) for i, block in enumerate(blocks)
    ]
    for copy in made:
        copy.start()
    for copy in made:
        copy.wait()


def stack(blocks):
    return pl.pallas_call(
        stack_kernel,
        out_shape=jax.ShapeDtypeStruct((len(blocks),) + blocks[0].shape, blocks[0].dtype),
        in_specs=[pl.BlockSpec(memory_space=pl.ANY)] * len(blocks),
        out_specs=pl.BlockSpec(memory_space=pl.ANY),
        scratch_shapes=[pltpu.SemaphoreType.DMA((len(blocks),))],
        compiler_params=pltpu.CompilerParams(vmem_limit_bytes=1024 * 1024),
        cost_estimate=pl.CostEstimate(flops=0, bytes_accessed=1024, transcendentals=0),
        name="stack",
    )(*blocks)


def first_layer_kernel(patches, places, hidden, gain, weights, out, mixed):
    @pl.when(places[3] == 0)
    def _():
        layer_kernel(patches, hidden, gain, weights, out, mixed)

    @pl.when(places[3] != 0)
    def _():
        out[...] = jnp.zeros_like(out)


def layer_kernel(patches, hidden, gain, weights, out, mixed):
    rows, width = hidden.shape
    heads = width // HEAD
    widened = hidden[...].astype(jnp.float32)
    normed = widened * lax.rsqrt(jnp.mean(widened * widened, -1, keepdims=True) + 1e-06)
    normed = (normed * gain[...].astype(jnp.float32)).astype(jnp.bfloat16)
    normed_a, normed_b = reorder(normed, "a"), reorder(normed, "b")
    tiles = [(at, min(256, width - at)) for at in range(0, width, 256)]

    def dot(left, right):
        return jnp.dot(left, right, preferred_element_type=jnp.float32)

    query, key, value = [], [], []
    for at, size in tiles:
        for matrix, left, parts in ((0, normed_a, query), (1, normed_b, key), (2, normed_a, value)):
            product = dot(left, weights[matrix, :, at : at + size]).astype(jnp.bfloat16)
            parts.extend(product[:, i : i + HEAD] for i in range(0, size, HEAD))
    scores = jnp.stack(
        [
            lax.dot_general(q, k, (((1,), (1,)), ((), ())), preferred_element_type=jnp.float32)
            for q, k in zip(query, key)
        ]
    ) * HEAD ** (-0.5)
    if rows != patches:
        row_image = lax.broadcasted_iota(jnp.int32, (rows, rows), 0) // patches
        column_image = lax.broadcasted_iota(jnp.int32, (rows, rows), 1) // patches
        scores = jnp.where((row_image == column_image)[None], scores, -jnp.inf)
    raised = jnp.exp(scores - jnp.max(scores, -1, keepdims=True))
    shares = (raised / jnp.sum(raised, -1, keepdims=True)).astype(jnp.bfloat16)
    for head in range(heads):
        mixed[:, head * HEAD : head * HEAD + HEAD] = dot(shares[head], value[head]).astype(
            jnp.bfloat16
        )
    mixed_b = reorder(mixed[...], "b")
    for at, size in tiles:
        added = dot(mixed_b, weights[3, :, at : at + size])
        out[:, at : at + size] = (
            hidden[:, at : at + size].astype(jnp.float32) + added
        ).astype(jnp.bfloat16)


def run_layer(stage, places, hidden, gain_row, weights, patches):
    rows, width = hidden.shape
    vmem = pl.BlockSpec(memory_space=pltpu.VMEM)
    weights = pltpu.with_memory_space_constraint(weights, pltpu.VMEM)
    kernel = first_layer_kernel if stage == 0 else layer_kernel
    scalars = (places,) if stage == 0 else ()
    return pl.pallas_call(
        functools.partial(kernel, patches),
        out_shape=jax.ShapeDtypeStruct((rows, width), jnp.bfloat16),
        in_specs=[pl.BlockSpec(memory_space=pltpu.SMEM)] * len(scalars) + [vmem] * 3,
        out_specs=vmem,
        scratch_shapes=[pltpu.VMEM((rows, width), jnp.bfloat16)],
        compiler_params=pltpu.CompilerParams(vmem_limit_bytes=12 * 1024 * 1024),
        cost_estimate=pl.CostEstimate(
            flops=8 * rows * width * width,
            bytes_accessed=4 * rows * width,
            transcendentals=rows * rows * width // HEAD,
        ),
        name="layer",
    )(*scalars, hidden, gain_row, weights)


def diagonal(size):
    row = lax.broadcasted_iota(jnp.int32, (size, size), 0)
    return row == lax.broadcasted_iota(jnp.int32, (size, size), 1)


def embed_kernel(spans, places, gain, weight, text_squares, *refs):
    parts, (embedded, squares) = refs[:-2], refs[-2:]
    rows, columns = embedded.shape
    values = []
    for first, count in spans:
        own, left, right, *forwarded = (part[...] for part in parts[first : first + count])
        halves = jnp.concatenate(forwarded, 0)
        total = jnp.where(places[3] == 0, left, jnp.where(places[3] == 1, halves, right))
        values.append(jnp.where(places[3] == SECTIONS - 1, own, total).astype(jnp.float32))
    values = jnp.concatenate(values, 0)
    centered = values - jnp.mean(values, -1, keepdims=True)
    variance = jnp.mean(centered * centered, -1, keepdims=True)
    normed = centered * lax.rsqrt(variance + 1e-05) * gain[...].astype(jnp.float32)
    normed = normed.astype(jnp.bfloat16)
    total = jnp.zeros((rows, 1), jnp.float32)
    for at in range(0, columns, 256):
        projected = jnp.dot(
            normed, weight[:, at : at + 256], preferred_element_type=jnp.float32
        )
        part = (0.5 * projected * (1.0 + lax.erf(projected * 0.5**0.5))).astype(jnp.bfloat16)
        embedded[:, at : at + 256] = part
        part = part.astype(jnp.float32)
        total = total + jnp.sum(part * part, -1, keepdims=True)
    squares[:, :rows] = jnp.sum(jnp.where(diagonal(rows), total, 0.0), 0, keepdims=True)
    squares[:, rows:] = text_squares[...]


def run_embed(places, pieces, gain_row, weight, text_squares):
    rows, columns = sum(piece[0].shape[0] for piece in pieces), weight.shape[1]
    parts = sum(pieces, ())
    firsts = [sum(len(piece) for piece in pieces[:i]) for i in range(len(pieces))]
    spans = [(first, len(piece)) for first, piece in zip(firsts, pieces)]
    vmem = pl.BlockSpec(memory_space=pltpu.VMEM)
    return pl.pallas_call(
        functools.partial(embed_kernel, spans),
        out_shape=(
            jax.ShapeDtypeStruct((rows, columns), jnp.bfloat16),
            jax.ShapeDtypeStruct((1, rows + text_squares.shape[1]), jnp.float32),
        ),
        in_specs=[pl.BlockSpec(memory_space=pltpu.SMEM)] + [vmem] * (3 + len(parts)),
        out_specs=(vmem, vmem),
        compiler_params=pltpu.CompilerParams(vmem_limit_bytes=12 * 1024 * 1024),
        name="embed",
    )(places, gain_row, weight, text_squares, *parts)


def place_kernel(patches, positions, counts, text, embedded, gain, *refs):
    squares, out = refs[:-1], refs[-1]
    length = text.shape[0]
    rows = embedded.shape[0]
    total = squares[0][...]
    for part in squares[1:]:
        total = total + part[...]
    scales = lax.rsqrt(total / LV + 1e-06)
    columns = []
    for first in range(0, scales.shape[1], rows):
        part = jnp.where(diagonal(rows), scales[:, first : first + rows], 0.0)
        columns.append(jnp.sum(part, 1, keepdims=True))
    gain_row = gain[...].astype(jnp.float32)

    def scale(values, column):
        return (values.astype(jnp.float32) * column * gain_row).astype(jnp.bfloat16)

    scaled = scale(embedded[...], columns[0])
    at = lax.broadcasted_iota(jnp.int32, (length, patches), 0)
    patch = lax.broadcasted_iota(jnp.int32, (length, patches), 1)
    one_row = lax.broadcasted_iota(jnp.int32, (length, 1), 0)
    picks, taken = [], None
    for slot in range(rows // patches):
        start, here = positions[0, slot], counts[0, slot] == 1
        picks.append(jnp.where((at == patch + start) & here, 1.0, 0.0).astype(jnp.bfloat16))
        inside = (one_row >= start) & (one_row < start + patches) & here
        taken = inside if taken is None else taken | inside
    placed = jnp.dot(
        jnp.concatenate(picks, 1), scaled, preferred_element_type=jnp.float32
    ).astype(jnp.bfloat16)
    out[...] = jnp.where(taken, placed, scale(text[...], jnp.concatenate(columns[1:], 0)))


def run_place(positions, counts, text, embedded, gain_row, squares, patches):
    vmem = pl.BlockSpec(memory_space=pltpu.VMEM)
    smem = pl.BlockSpec(memory_space=pltpu.SMEM)
    return pl.pallas_call(
        functools.partial(place_kernel, patches),
        out_shape=jax.ShapeDtypeStruct(text.shape, jnp.bfloat16),
        in_specs=[smem, smem] + [vmem] * (3 + len(squares)),
        out_specs=vmem,
        compiler_params=pltpu.CompilerParams(vmem_limit_bytes=12 * 1024 * 1024),
        name="place",
    )(positions, counts, text, embedded, gain_row, *squares)


def on_device(
    images, counts, positions, text_rows, norm_gain, w_qkv, w_out, proj_gain, proj_weight, llm_gain
):
    section = lax.axis_index("section")
    place = lax.axis_index("dp")
    core = place % NC
    x_place = (place // NC) % NX
    z_place = (place // (NC * NX)) % NZ
    y_place = place // (NC * NX * NZ)
    width = w_out.shape[2]
    micro, patches = images.shape[1], images.shape[2]

    places = jnp.stack([core, x_place, y_place, section]).astype(jnp.int32)

    text = text_rows[0].astype(jnp.float32)
    text_squares = jnp.sum(text * text, -1)[None]

    is_first = core == 0
    is_low = z_place == 0
    parts = [w_qkv[0][:, i * width : (i + 1) * width] for i in range(3)] + [w_out[0]]
    keep = jnp.concatenate([jnp.where(is_first, parts[i], parts[i + 2]) for i in (0, 1)], 1)
    give = jnp.concatenate([jnp.where(is_first, parts[i + 2], parts[i]) for i in (0, 1)], 1)
    got = dp_permute(give, dc=1)
    pair = jnp.concatenate([jnp.where(is_first, keep, got), jnp.where(is_first, got, keep)], 0)
    other = dp_permute(pair, dz=1)
    quad = jnp.concatenate([jnp.where(is_low, pair, other), jnp.where(is_low, other, pair)], 0)
    line_a, line_b = gather_lines(quad[:, :width], quad[:, width:], places)
    half = line_a.shape[0] // 2
    top, low = slice(0, half), slice(half, None)
    mine_a, onward_a = ring(line_a, "dy", top, low)
    mine_b, onward_b = ring(line_b, "dx", top, low)
    mine = (mine_a, mine_b)
    early = [images[0, i] for i in range(micro)]
    early += [norm_gain[0].reshape(1, width), proj_gain.reshape(1, width), llm_gain.reshape(1, -1)]
    places, text_squares, *early = lax.optimization_barrier((places, text_squares, *early))
    pieces, (gain_row, proj_gain_row, llm_gain_row) = early[:micro], early[micro:]
    near = sum((part[:3] for part in mine), ())
    near = lax.optimization_barrier((near, onward_a, onward_b))[0]
    line = line_a.shape[0]
    plan = ((0, 0, line), (1, 0, line), (3, 0, line))
    swapped = dp_permute(stack(near), dc=1)
    weights = hold_weights((swapped,) + near, plan, (1, 0), places)
    far = sum((part[3:] for part in mine), ())
    last_far, weights = lax.optimization_barrier((far[0], weights))
    far = (last_far,) + far[1:]
    far = far + tuple(dp_permute(part, dc=1) for part in far)
    weights = hold_weights(far, ((2, 0, half), (2, half, half)), (0, 1), places, weights)

    last = SECTIONS - 1
    for stage in range(SECTIONS):
        moved = []
        for hidden in pieces:
            hidden = run_layer(stage, places, hidden, gain_row, weights, patches)
            if stage < last:
                moved.append(section_permute(hidden, [(stage, stage + 1)]))
            else:
                left = section_permute(hidden, [(last, 0)])
                right = section_permute(hidden, [(last, last - 1)])
                moved.append((hidden, left, right))
        pieces = moved
    finished = pieces[-1][0]
    for i, (hidden, left, right) in enumerate(pieces):
        left, right, finished = lax.optimization_barrier((left, right, finished))
        if i + 1 < micro:
            forwarded = (section_permute(right, [(last - 1, 1)]),)
        else:
            cut = hidden.shape[0] // 4
            top = section_permute(left[:cut], [(0, 1)])
            forwarded = (top, section_permute(right[cut:], [(last - 1, 1)]))
        pieces[i] = (hidden, left, right) + forwarded
    pieces[-1] = (finished,) + pieces[-1][1:]
    embedded, squares = run_embed(places, pieces, proj_gain_row, proj_weight, text_squares)
    others = [
        section_permute(squares, [(i, (i + by) % SECTIONS) for i in range(SECTIONS)])
        for by in range(1, SECTIONS)
    ]
    out = run_place(
        positions, counts, text_rows[0], embedded, llm_gain_row, [squares] + others, patches
    )
    return out[None]


def solution(mesh):
    in_specs = (
        P("dp", None, None, None),
        P("dp", None),
        P("dp", None),
        P("dp", None, "section"),
        P("section", None),
        P("section", "dp", None),
        P("section", "dp", None),
        P(),
        P(None, "section"),
        P("section"),
    )
    out_specs = P("dp", None, "section")
    return jax.shard_map(
        on_device, mesh=mesh, in_specs=in_specs, out_specs=out_specs, check_vma=False
    )
```
